512 devices in a mesh: train: 32 (over x, z_lo), query: 16 (over z_hi, y, core).
Axes of the slice: x: 4, y: 4, z: 16 (z_hi: 2, z_lo: 8; z = z_hi * 8 + z_lo), core: 2. Of those that a mesh axis runs over, the one named last changes fastest.
Arguments:
- train_factors: bfloat16 [32768, 16, 128], P(('train', 'query'))
- query_factors: bfloat16 [8192, 16, 128], P(('query', 'train'))
Outputs:
- scores: float32 [32768, 8192], P('train', 'query')
All inputs are finite; a program needn't handle non-finite values.
Results may differ from the reference program's by a relative error of at most 0.0041.
Values may be sent and summed in bfloat16 or wider, within the bound.
A program may use at most 128 MiB of HBM per device.

```python
import jax
import jax.numpy as jnp
from jax import lax

R = 64
SEQ = 16
NTR = 32768
NQ = 8192


def draw_train_factors(key, part):
    key = jax.random.fold_in(key, 11)
    first, second, third = jax.random.split(key, 3)
    base = jax.random.normal(first, (NTR, SEQ, 2 * R), jnp.float32)
    spread = 0.25
    position = jnp.arange(NTR, dtype=jnp.float32) / NTR
    seq_scale = 10.0 ** (0.25 * position + spread * jax.random.uniform(second, (NTR,), jnp.float32))
    col_scale = 10.0 ** (0.5 * jax.random.uniform(third, (2 * R,), jnp.float32))
    return (base * seq_scale[:, None, None] * col_scale[None, None, :]).astype(jnp.bfloat16)


def draw_query_factors(key, part):
    key = jax.random.fold_in(key, 23)
    first, second, third = jax.random.split(key, 3)
    base = jax.random.normal(first, (NQ, SEQ, 2 * R), jnp.float32)
    spread = 0.3
    seq_scale = 10.0 ** (spread * jax.random.uniform(second, (NQ,), jnp.float32))
    col_scale = 10.0 ** (0.5 * jax.random.uniform(third, (2 * R,), jnp.float32))
    return (base * seq_scale[:, None, None] * col_scale[None, None, :]).astype(jnp.bfloat16)


def setup_inputs(seed: int = 0) -> dict:
    splits = jax.random.split(jax.random.key(seed), 3)
    train_factors = draw_train_factors(jax.random.fold_in(splits[2], 71), 0)
    query_factors = draw_query_factors(jax.random.fold_in(splits[2], 71), 0)
    return {"train_factors": train_factors, "query_factors": query_factors}


def sequence_grads(factors):
    first = factors[:, :, :R].astype(jnp.float32)
    second = factors[:, :, R:].astype(jnp.float32)
    return jnp.einsum('sti,stj->sij', first, second, precision=lax.Precision.HIGHEST) / SEQ

def inverse_of(cov):
    damped = cov + 0.1 * (jnp.trace(cov) / R) * jnp.eye(R, dtype=jnp.float32)
    lower = jnp.linalg.cholesky(damped)
    return jax.scipy.linalg.cho_solve((lower, True), jnp.eye(R, dtype=jnp.float32))

def precondition_factors(factors, inv_in, inv_out):
    count = factors.shape[0]
    first = factors[:, :, :R].reshape(count * SEQ, R).astype(jnp.float32)
    second = factors[:, :, R:].reshape(count * SEQ, R).astype(jnp.float32)
    left = jnp.dot(first, inv_in, precision=lax.Precision.HIGHEST).reshape(count, SEQ, R)
    right = jnp.dot(second, inv_out, precision=lax.Precision.HIGHEST).reshape(count, SEQ, R)
    return jnp.einsum('sti,stj->sij', left, right, precision=lax.Precision.HIGHEST) / SEQ

def reference(train_factors, query_factors):
    train_grads = sequence_grads(train_factors).reshape(NTR, R * R).astype(jnp.bfloat16)
    first = train_factors[:, :, :R].reshape(NTR * SEQ, R).astype(jnp.float32)
    second = train_factors[:, :, R:].reshape(NTR * SEQ, R).astype(jnp.float32)
    cov_in = jnp.dot(first.T, first, precision=lax.Precision.HIGHEST) / (NTR * SEQ)
    cov_out = jnp.dot(second.T, second, precision=lax.Precision.HIGHEST) / (NTR * SEQ)
    inv_in = inverse_of(cov_in)
    inv_out = inverse_of(cov_out)
    query_pre = precondition_factors(query_factors, inv_in, inv_out)
    query_pre = query_pre.reshape(NQ, R * R).astype(jnp.bfloat16)
    product = lax.dot_general(train_grads.astype(jnp.float32), query_pre.astype(jnp.float32), (((1,), (1,)), ((), ())), preferred_element_type=jnp.float32)
    return product * 0.125
```

```python
import functools

import jax
import jax.numpy as jnp
from jax import lax
from jax.experimental import pallas as pl
from jax.experimental.pallas import tpu as pltpu
from jax.sharding import PartitionSpec as P

MESH = pl.DeviceIdType.MESH
F32 = jnp.float32
BF16 = jnp.bfloat16

NX, NY, NZ, ZLO = 4, 4, 16, 8
UNIT = 256
NEWTON = 8


def coordinates():
    t = lax.axis_index("train")
    q = lax.axis_index("query")
    return t // ZLO, (q // 2) % NY, (q // (2 * NY)) * ZLO + t % ZLO, q % 2


def device(x, y, z, c):
    return (x * ZLO + z % ZLO, (z // ZLO) * (2 * NY) + y * 2 + c)


def iota(shape, dim):
    return lax.broadcasted_iota(jnp.int32, shape, dim)


def split2(v):
    hi = v.astype(BF16)
    return hi, (v - hi.astype(F32)).astype(BF16)


def mm(a, b):
    return jnp.dot(a, b, preferred_element_type=F32)


def mm3(a, b):
    ah, al = split2(a)
    bh, bl = split2(b)
    return mm(ah, bh) + (mm(ah, bl) + mm(al, bh))


def mmh(a, b):
    return jnp.dot(a, b, preferred_element_type=F32, precision=lax.Precision.HIGHEST)


def inverse_pair(total, tokens):
    row, lane = iota((64, 128), 0), iota((64, 128), 1)
    cov = total * (1.0 / tokens)
    first = lane < 64
    tr_in = jnp.sum(jnp.where(lane == row, cov, 0.0)) * (1.0 / 64)
    tr_out = jnp.sum(jnp.where(lane == row + 64, cov, 0.0)) * (1.0 / 64)
    top = jnp.where(first, cov + jnp.where(lane == row, 0.1 * tr_in, 0.0), 0.0)
    bottom = jnp.where(first, 0.0, cov + jnp.where(lane == row + 64, 0.1 * tr_out, 0.0))
    damped = jnp.concatenate([top, bottom], axis=0)
    r, l = iota((128, 128), 0), iota((128, 128), 1)
    eye = jnp.where(r == l, 1.0, 0.0)
    low, high = 0.1, 64.1
    seed = 2.0 / (low + high)
    inv = jnp.where(r == l, jnp.where(r < 64, seed / tr_in, seed / tr_out), 0.0)
    bound = 2.0 * low / (low + high)
    for step in range(NEWTON):
        mul = mmh if step >= NEWTON - 2 else mm3
        mapped = bound * (2.0 - bound)
        scale = 2.0 / (1.0 + mapped) if step < NEWTON - 2 else 1.0
        inv = scale * mul(inv, 2.0 * eye - mul(damped, inv))
        bound = 2.0 * mapped / (1.0 + mapped)
    return inv


def expand(first_t, mask):
    base = jnp.concatenate([first_t[:32], first_t[32:]], axis=1)
    rows = [jnp.broadcast_to(base[i : i + 1], (8, 256)) * mask for i in range(32)]
    return jnp.concatenate(rows, axis=0).astype(BF16)


def spread(second, rolled, group):
    left = iota((128, 128), 1) < 64
    if group == 0:
        return jnp.concatenate([jnp.where(left, second, 0.0), jnp.where(left, 0.0, rolled)], axis=0)
    return jnp.concatenate([jnp.where(left, rolled, 0.0), jnp.where(left, 0.0, second)], axis=0)


def store_rows(out_ref, row, pair, scale):
    a, b = pair
    for i in range(32):
        tile = jnp.concatenate([a[8 * i : 8 * i + 8], b[8 * i : 8 * i + 8]], axis=0) * scale
        out_ref[pl.ds(row, 16), 128 * i : 128 * i + 128] = tile.astype(BF16)


def kernel(
    tokens, train_ref, query_ref, out_ref, tbuf, qbuf, grads, pre, part, sibpart, half, rs, zs, ag, total,
    sib_s, sib_r, small_s, small_r, tz_s, tz_r, ty_s, ty_r, tzy_s, tzy_r, tc_s, tc_r, qq_s, qq_r, qx_s, qx_r,
):
    x, y, z, c = coordinates()
    me_t = lax.axis_index("train")
    me_q = lax.axis_index("query")
    plane = x * NY + y
    sibling = device(x, y, z, 1 - c)
    plane_peers = [
        (lax.rem(x + dx, NX), lax.rem(y + dy, NY)) for dx in range(NX) for dy in range(NY) if dx or dy
    ]
    z_peers = [lax.rem(z + dz, NZ) for dz in range(1, NZ)]

    barrier = pltpu.get_barrier_semaphore()
    for pz in z_peers:
        pl.semaphore_signal(barrier, inc=1, device_id=device(x, y, pz, c), device_id_type=MESH)
    for px, py in plane_peers:
        pl.semaphore_signal(barrier, inc=1, device_id=device(px, py, z, c), device_id_type=MESH)
    pl.semaphore_signal(barrier, inc=1, device_id=sibling, device_id_type=MESH)

    left = iota((128, 128), 1) < 64

    def arrange(src, at, dst, block, to):
        a = src[pl.ds(at, 128), :]
        b = src[pl.ds(at + 128, 128), :]
        a32, b32 = a.astype(F32), b.astype(F32)
        at32, bt32 = a32.T, b32.T
        dst[block, pl.ds(to, 64), :] = at32[:64].astype(BF16)
        dst[block, pl.ds(to + 64, 64), :] = bt32[:64].astype(BF16)
        dst[block, pl.ds(to + 128, 128), :] = jnp.where(left, pltpu.roll(a32, 64, 1), b32).astype(BF16)
        return a, b, at32.astype(BF16), bt32.astype(BF16)

    cov = jnp.zeros((128, 128), F32)
    for u in range(4):
        a, b, at, bt = arrange(train_ref, u * UNIT, tbuf, me_q, u * UNIT)
        cov = cov + mm(at, a) + mm(bt, b)
    arrange(query_ref, 0, qbuf, me_t, 0)
    part[...] = jnp.where(iota((64, 128), 1) < 64, cov[:64], cov[64:])

    pl.semaphore_wait(barrier, 31)

    sends = []

    def send(src, dst, ssem, rsem, to):
        cp = pltpu.make_async_remote_copy(
            src_ref=src, dst_ref=dst, send_sem=ssem, recv_sem=rsem, device_id=to, device_id_type=MESH
        )
        cp.start()
        sends.append(cp)
        return cp

    def arrived(dst, ssem, rsem):
        pltpu.make_async_remote_copy(
            src_ref=dst, dst_ref=dst, send_sem=ssem, recv_sem=rsem, device_id=sibling, device_id_type=MESH
        ).wait_recv()

    pair = send(part, sibpart, sib_s, sib_r, sibling)
    far = lax.rem(z + 8, NZ)
    far_q = lax.rem(me_q + 8, 16)

    def rows(block, h):
        return tbuf.at[block, pl.ds(512 * h, 512)]

    def far_send(h):
        return send(rows(me_q, h), rows(me_q, h), tz_s.at[h], tz_r.at[h], device(x, y, far, c))

    first_far = far_send(0)
    zlo = lax.rem(z, ZLO)
    zbase = z - zlo
    quad = zlo - lax.rem(zlo, 4)

    def quad_peer(d):
        return quad + lax.rem(zlo + d, 4)

    def unit_send(block, sem, to):
        return send(qbuf.at[block], qbuf.at[block], qq_s.at[sem], qq_r.at[sem], device(x, y, zbase + to, c))

    partner = lax.rem(zlo + 4, ZLO)
    unit_send(me_t, 3, partner)
    for d in (1, 2, 3):
        unit_send(me_t, d - 1, quad_peer(d))
    for dy in (1, 2, 3):
        send(tbuf.at[me_q], tbuf.at[me_q], ty_s.at[dy - 1], ty_r.at[dy - 1], device(x, lax.rem(y + dy, NY), z, c))
    send(tbuf.at[me_q], tbuf.at[me_q], tc_s.at[0], tc_r.at[0], sibling)

    pair.wait_recv()
    mine = part[...] + sibpart[...]
    for k in range(16):
        half[k] = mine[4 * k : 4 * k + 4]

    def small(stage, src_of, dst, slot, peers):
        for src, to in zip(src_of, peers, strict=True):
            pltpu.make_async_remote_copy(
                src_ref=src, dst_ref=dst.at[slot], send_sem=small_s.at[stage], recv_sem=small_r.at[stage],
                device_id=to, device_id_type=MESH,
            ).start()

    def small_wait(stage, buf, recv):
        w = pltpu.make_async_remote_copy(
            src_ref=buf.at[pl.ds(0, 15)], dst_ref=buf.at[pl.ds(0, 15)], send_sem=small_s.at[stage],
            recv_sem=small_r.at[stage], device_id=sibling, device_id_type=MESH,
        )
        if recv:
            w.wait_recv()
        else:
            w.wait_send()

    plane_to = [device(px, py, z, c) for px, py in plane_peers]
    small(0, [half.at[px * NY + py] for px, py in plane_peers], rs, plane, plane_to)
    rs[plane] = half[plane]

    mask = jnp.where(iota((8, 256), 1) // 16 % 8 == iota((8, 256), 0), 1.0, 0.0)

    def form_unit(block, u):
        at = pl.multiple_of(u * UNIT, UNIT)
        second = tbuf[block, pl.ds(at + 128, 128), :].astype(F32)
        rolled = pltpu.roll(second, 64, 1)
        outs = []
        for g in range(2):
            lhs = expand(tbuf[block, pl.ds(at + 64 * g, 64), :].astype(F32), mask)
            outs.append(mm(lhs, spread(second, rolled, g).astype(BF16)))
        row = pl.multiple_of(block * 64 + u * 16, 16)
        store_rows(grads, row, outs, 1.0 / 16)

    def form(blocks, lo, hi):
        for block in blocks:

            @pl.loop(lo, hi)
            def _(u, block=block):
                form_unit(block, u)

    own = [me_q - 2 * y + 2 * lax.rem(y + dy, NY) for dy in range(NY)]
    from_y = [me_q - 2 * y + 2 * lax.rem(y + NY - dy, NY) for dy in range(NY)]
    far_from_y = [lax.rem(b + 8, 16) for b in from_y]

    def other(block):
        return block + 1 - 2 * c

    form([me_q], 0, 4)

    small_wait(0, rs, True)
    piece = rs[0]
    for k in range(1, 16):
        piece = piece + rs[k]
    zs[z] = piece
    small(1, [zs.at[z]] * 15, zs, z, [device(x, y, pz, c) for pz in z_peers])

    arrived(qbuf.at[me_t], qq_s.at[3], qq_r.at[3])
    partner_t = me_t - zlo + partner
    for d in (1, 2, 3):
        unit_send(partner_t, 3 + d, quad_peer(d))
    arrived(tbuf.at[me_q], tc_s.at[0], tc_r.at[0])
    form([other(me_q)], 0, 4)
    for dy in (1, 2, 3):
        arrived(tbuf.at[me_q], ty_s.at[dy - 1], ty_r.at[dy - 1])
        send(tbuf.at[from_y[dy]], tbuf.at[from_y[dy]], tc_s.at[dy], tc_r.at[dy], sibling)
    form([from_y[1]], 0, 4)

    small_wait(1, zs, True)
    piece = zs[0]
    for k in range(1, 16):
        piece = piece + zs[k]
    ag[plane] = piece
    small(2, [ag.at[plane]] * 15, ag, plane, plane_to)

    first_far.wait_send()
    far_send(1)
    for d in (1, 2, 3):
        arrived(qbuf.at[me_t], qq_s.at[d - 1], qq_r.at[d - 1])

    def x_send(s, at):
        src = qbuf.at[pl.ds(x * ZLO + at, 4)]
        for dx in (1, 2, 3):
            send(src, src, qx_s.at[3 * s + dx - 1], qx_r.at[3 * s + dx - 1], device(lax.rem(x + dx, NX), y, z, c))

    x_send(0, quad)
    form([from_y[2]], 0, 4)

    small_wait(2, ag, True)
    for k in range(16):
        total[4 * k : 4 * k + 4] = ag[k]
    inv = inverse_pair(total[...], tokens)

    def far_recv(h):
        arrived(rows(me_q, h), tz_s.at[h], tz_r.at[h])
        for dy in (1, 2, 3):
            i = 3 * h + dy - 1
            send(
                rows(far_q, h), rows(far_q, h), tzy_s.at[i], tzy_r.at[i], device(x, lax.rem(y + dy, NY), z, c)
            )
        send(rows(far_q, h), rows(far_q, h), tc_s.at[4 + h], tc_r.at[4 + h], sibling)

    far_recv(0)
    for d in (1, 2, 3):
        arrived(qbuf.at[me_t], qq_s.at[3 + d], qq_r.at[3 + d])
    x_send(1, 4 - quad)
    form([from_y[3]], 0, 4)
    for dy in (1, 2, 3):
        arrived(tbuf.at[me_q], tc_s.at[dy], tc_r.at[dy])
    form([other(b) for b in from_y[1:]], 0, 4)

    in_parts, out_parts = [], []
    lane64 = iota((64, 128), 1) < 64
    top, bottom = inv[:64], inv[64:]
    w_in = jnp.concatenate([top, pltpu.roll(top, 64, 1)], axis=0)
    w_out = jnp.concatenate([pltpu.roll(bottom, 64, 1), bottom], axis=0)
    in_h, in_l = split2(w_in)
    out_h, out_l = split2(w_out)

    for s in range(2):
        for dx in (1, 2, 3):
            arrived(qbuf.at[pl.ds(0, 4)], qx_s.at[3 * s + dx - 1], qx_r.at[3 * s + dx - 1])

    @pl.loop(0, 32)
    def _(b):
        first = qbuf[b, pl.ds(0, 128), :]
        second = qbuf[b, pl.ds(128, 128), :]
        first_p = mm(in_h, first) + mm(in_l, first)
        second_p = mm(second, out_h) + mm(second, out_l)
        rolled = pltpu.roll(second_p, 64, 1)
        outs = []
        for g in range(2):
            part_t = first_p[64 * g : 64 * g + 64]
            hi = part_t.astype(BF16).astype(F32)
            lhs_h = expand(hi, mask)
            lhs_l = expand(part_t - hi, mask)
            rhs = spread(second_p, rolled, g)
            rhs_h, rhs_l = split2(rhs)
            outs.append(mm(lhs_h, rhs_h) + (mm(lhs_h, rhs_l) + mm(lhs_l, rhs_h)))
        store_rows(pre, pl.multiple_of(b * 16, 16), outs, 1.0 / 16)

    far_recv(1)

    def product(zhi):
        for m in range(2):
            for n in range(2):
                at = pl.multiple_of(zhi * 512 + m * 256, 256)
                tile = lax.dot_general(
                    grads[pl.ds(at, 256), :], pre[256 * n : 256 * n + 256, :], (((1,), (1,)), ((), ())),
                    preferred_element_type=F32,
                )
                out_ref[pl.ds(at, 256), 256 * n : 256 * n + 256] = tile * 0.125

    zhi = z // ZLO
    product(zhi)

    for h in range(2):
        for dy in (1, 2, 3):
            i = 3 * h + dy - 1
            arrived(rows(me_q, h), tzy_s.at[i], tzy_r.at[i])
            b = far_from_y[dy]
            send(rows(b, h), rows(b, h), tc_s.at[6 + i], tc_r.at[6 + i], sibling)
        form(far_from_y, 2 * h, 2 * h + 2)
        arrived(rows(me_q, h), tc_s.at[4 + h], tc_r.at[4 + h])
        for dy in (1, 2, 3):
            i = 3 * h + dy - 1
            arrived(rows(me_q, h), tc_s.at[6 + i], tc_r.at[6 + i])
        form([other(b) for b in far_from_y], 2 * h, 2 * h + 2)
    product(1 - zhi)

    for cp in sends:
        if cp is not first_far:
            cp.wait_send()
    small_wait(0, rs, False)
    small_wait(1, zs, False)
    small_wait(2, ag, False)


def body(train_factors, query_factors):
    tokens = train_factors.shape[0] * train_factors.shape[1] * 512
    train = train_factors.reshape(-1, 128)
    query = query_factors.reshape(-1, 128)
    vmem = pl.BlockSpec(memory_space=pltpu.VMEM)
    dma = pltpu.SemaphoreType.DMA
    return pl.pallas_call(
        functools.partial(kernel, tokens),
        out_shape=jax.ShapeDtypeStruct((1024, 512), F32),
        in_specs=[vmem, vmem],
        out_specs=vmem,
        scratch_shapes=[
            pltpu.VMEM((16, 1024, 128), BF16),
            pltpu.VMEM((32, 256, 128), BF16),
            pltpu.VMEM((1024, 4096), BF16),
            pltpu.VMEM((512, 4096), BF16),
            pltpu.VMEM((64, 128), F32),
            pltpu.VMEM((64, 128), F32),
            pltpu.VMEM((16, 4, 128), F32),
            pltpu.VMEM((16, 4, 128), F32),
            pltpu.VMEM((16, 4, 128), F32),
            pltpu.VMEM((16, 4, 128), F32),
            pltpu.VMEM((64, 128), F32),
            dma, dma, dma((3,)), dma((3,)), dma((2,)), dma((2,)), dma((3,)), dma((3,)), dma((6,)), dma((6,)),
            dma((12,)), dma((12,)), dma((7,)), dma((7,)), dma((6,)), dma((6,)),
        ],
        compiler_params=pltpu.CompilerParams(
            collective_id=0, has_side_effects=True, vmem_limit_bytes=48 * 2**20
        ),
        name="influence",
    )(train, query)


def solution(mesh):
    return jax.shard_map(
        body,
        mesh=mesh,
        in_specs=(P(("train", "query"), None, None), P(("query", "train"), None, None)),
        out_specs=P("train", "query"),
        check_vma=False,
    )
```

```python
import functools

import jax
import jax.numpy as jnp
from jax import lax
from jax.experimental import pallas as pl
from jax.experimental.pallas import tpu as pltpu
from jax.sharding import PartitionSpec as P

MESH = pl.DeviceIdType.MESH
F32 = jnp.float32
BF16 = jnp.bfloat16

NX, NY, NZ, ZLO = 4, 4, 16, 8
UNIT = 256
HALF = 512
STAGE = 32
CHUNKS = 2
NEWTON = 8
LOW, HIGH = 0.1, 64.1


def coordinates():
    t = lax.axis_index("train")
    q = lax.axis_index("query")
    return t // ZLO, (q // 2) % NY, (q // (2 * NY)) * ZLO + t % ZLO, q % 2


def device(x, y, z, c):
    return (x * ZLO + z % ZLO, (z // ZLO) * (2 * NY) + y * 2 + c)


def iota(shape, dim):
    return lax.broadcasted_iota(jnp.int32, shape, dim)


def split2(v):
    hi = v.astype(BF16)
    return hi, (v - hi.astype(F32)).astype(BF16)


def mm(a, b):
    return jnp.dot(a, b, preferred_element_type=F32)


def mm3(a, b):
    ah, al = split2(a)
    bh, bl = split2(b)
    return mm(ah, bh) + (mm(ah, bl) + mm(al, bh))


def mmh(a, b):
    return jnp.dot(a, b, preferred_element_type=F32, precision=lax.Precision.HIGHEST)


def eye128():
    return jnp.where(iota((128, 128), 0) == iota((128, 128), 1), 1.0, 0.0)


def damp(total, tokens):
    row, lane = iota((64, 128), 0), iota((64, 128), 1)
    cov = total * (1.0 / tokens)
    first = lane < 64
    tr_in = jnp.sum(jnp.where(lane == row, cov, 0.0)) * (1.0 / 64)
    tr_out = jnp.sum(jnp.where(lane == row + 64, cov, 0.0)) * (1.0 / 64)
    top = jnp.where(first, cov + jnp.where(lane == row, 0.1 * tr_in, 0.0), 0.0)
    bottom = jnp.where(first, 0.0, cov + jnp.where(lane == row + 64, 0.1 * tr_out, 0.0))
    r, lanes = iota((128, 128), 0), iota((128, 128), 1)
    mean = jnp.where(r < 64, tr_in, tr_out)
    guess = jnp.where(r == lanes, (2.0 / (LOW + HIGH)) / mean, 0.0)
    return jnp.concatenate([top, bottom], axis=0), guess


def newton(damped, inv, lo, hi):
    bound = 2.0 * LOW / (LOW + HIGH)
    for step in range(hi):
        mapped = bound * (2.0 - bound)
        plain = step >= NEWTON - 2
        if step >= lo:
            mul = mmh if plain else mm3
            inv = mul(inv, 2.0 * eye128() - mul(damped, inv))
            if not plain:
                inv = inv * (2.0 / (1.0 + mapped))
        bound = 2.0 * mapped / (1.0 + mapped)
    return inv


def expand(first_t, mask):
    rows = []
    for i in range(32):
        a = jnp.broadcast_to(first_t[i : i + 1], (8, 128)) * mask
        b = jnp.broadcast_to(first_t[32 + i : 33 + i], (8, 128)) * mask
        rows.append(jnp.concatenate([a, b], axis=1))
    return jnp.concatenate(rows, axis=0)


def spread(second, rolled, group):
    left = iota((128, 128), 1) < 64
    zero = jnp.zeros_like(second)
    if group == 0:
        return jnp.concatenate([jnp.where(left, second, zero), jnp.where(left, zero, rolled)], axis=0)
    return jnp.concatenate([jnp.where(left, rolled, zero), jnp.where(left, zero, second)], axis=0)


def store_rows(out_ref, row, pair):
    a, b = pair
    for i in range(32):
        tile = jnp.concatenate([a[8 * i : 8 * i + 8], b[8 * i : 8 * i + 8]], axis=0)
        out_ref[pl.ds(row, 16), 128 * i : 128 * i + 128] = tile.astype(BF16)


def kernel(
    tokens, train_hbm, query_hbm, out_ref, train_ref, query_ref, tbuf, qbuf, grads, pre, ppre, part, sibpart, half, rs, zs,
    ag, total, damped, inv, in_sem, sib_s, sib_r, small_s, small_r, ring_s, ring_r, ku_s, ku_r, kd_s, kd_r, x_s, x_r,
    y_s, y_r, fy_s, fy_r, c_s, c_r,
):
    x, y, z, c = coordinates()
    me_t = lax.axis_index("train")
    me_q = lax.axis_index("query")
    plane = x * NY + y
    sibling = device(x, y, z, 1 - c)
    zlo = lax.rem(z, ZLO)
    zhi = z // ZLO
    plane_peers = [
        (lax.rem(x + dx, NX), lax.rem(y + dy, NY)) for dx in range(NX) for dy in range(NY) if dx or dy
    ]
    plane_to = [device(px, py, z, c) for px, py in plane_peers]
    z_to = [device(x, y, lax.rem(z + dz, NZ), c) for dz in range(1, NZ)]
    x_to = [device(lax.rem(x + d, NX), y, z, c) for d in range(NX)]
    y_to = [device(x, lax.rem(y + d, NY), z, c) for d in range(NY)]

    inputs = [
        pltpu.make_async_copy(train_hbm, train_ref, in_sem.at[0]),
        pltpu.make_async_copy(query_hbm, query_ref, in_sem.at[1]),
    ]
    for cp in inputs:
        cp.start()
    barrier = pltpu.get_barrier_semaphore()
    for to in [*z_to, *plane_to, sibling]:
        pl.semaphore_signal(barrier, inc=1, device_id=to, device_id_type=MESH)
    for cp in inputs:
        cp.wait()

    left = iota((128, 128), 1) < 64

    def arrange(src, at, dst, block, to):
        a = src[pl.ds(at, 128), :]
        b = src[pl.ds(at + 128, 128), :]
        a32, b32 = a.astype(F32), b.astype(F32)
        at32, bt32 = a32.T, b32.T
        dst[block, pl.ds(to, 64), :] = at32[:64].astype(BF16)
        dst[block, pl.ds(to + 64, 64), :] = bt32[:64].astype(BF16)
        dst[block, pl.ds(to + 128, 128), :] = jnp.where(left, pltpu.roll(a32, 64, 1), b32).astype(BF16)
        return a, b, at32.astype(BF16), bt32.astype(BF16)

    cov = jnp.zeros((128, 128), F32)
    for u in range(4):
        a, b, at, bt = arrange(train_ref, u * UNIT, tbuf, 2 * me_q + u // 2, (u % 2) * UNIT)
        cov = cov + mm(at, a) + mm(bt, b)
    arrange(query_ref, 0, qbuf, me_t, 0)
    part[...] = jnp.where(iota((64, 128), 1) < 64, cov[:64], cov[64:])

    pl.semaphore_wait(barrier, 31)

    def copy(src, dst, ssem, rsem, to=sibling):
        return pltpu.make_async_remote_copy(
            src_ref=src, dst_ref=dst, send_sem=ssem, recv_sem=rsem, device_id=to, device_id_type=MESH
        )

    rows = HALF // CHUNKS

    def ring_index(d, step):
        return (step * 2 + d) * CHUNKS

    def ring_slot(d, step, k):
        landed = 2 * lax.rem(me_q + 8, 16) + d
        return tbuf.at[jnp.where(step < 7, STAGE + d * 7 + step, landed), pl.ds(rows * k, rows)]

    def ring_send(d, step, k, src):
        zr = lax.rem(z + (1 if d == 0 else NZ - 1), NZ)
        landed = 2 * ((1 - zr // ZLO) * 8 + 2 * y + c) + d
        dst = tbuf.at[jnp.where(step < 7, STAGE + d * 7 + step, landed), pl.ds(rows * k, rows)]
        i = ring_index(d, step) + k
        copy(src, dst, ring_s.at[i], ring_r.at[i], device(x, y, zr, c)).start()

    def ring_recv(d, step, k):
        i = ring_index(d, step) + k
        slot = ring_slot(d, step, k)
        copy(slot, slot, ring_s.at[i], ring_r.at[i]).wait_recv()
        return slot

    def chain_units(s):
        return me_t - jnp.minimum(s, zlo), me_t + jnp.minimum(s, ZLO - 1 - zlo)

    def chain_send(s):
        up, down = chain_units(s)

        @pl.when((zlo >= s) & (zlo < ZLO - 1))
        def _():
            to = device(x, y, jnp.minimum(z + 1, NZ - 1), c)
            copy(qbuf.at[up], qbuf.at[up], ku_s.at[s], ku_r.at[s], to).start()

        @pl.when((zlo + s <= ZLO - 1) & (zlo > 0))
        def _():
            to = device(x, y, jnp.maximum(z - 1, 0), c)
            copy(qbuf.at[down], qbuf.at[down], kd_s.at[s], kd_r.at[s], to).start()

    def chain_recv(s):
        up, down = chain_units(s)

        @pl.when(zlo >= s)
        def _():
            copy(qbuf.at[up], qbuf.at[up], ku_s.at[s - 1], ku_r.at[s - 1]).wait_recv()

        @pl.when(zlo + s <= ZLO - 1)
        def _():
            copy(qbuf.at[down], qbuf.at[down], kd_s.at[s - 1], kd_r.at[s - 1]).wait_recv()

    def x_send(unit):
        for d in (1, 2, 3):
            copy(qbuf.at[unit], qbuf.at[unit], x_s.at[d - 1], x_r.at[d - 1], x_to[d]).start()

    def block(b):
        return tbuf.at[pl.ds(2 * b, 2)]

    def near(e):
        other = e // 4
        return me_q - lax.rem(me_q, 8) + 2 * lax.rem(y + NY - lax.rem(e, 4), NY) + (c + other - 2 * c * other)

    def far(e):
        return lax.rem(near(e) + 8, 16)

    copy(part, sibpart, sib_s, sib_r).start()
    for k in range(CHUNKS):
        for d in range(2):
            ring_send(d, 0, k, tbuf.at[2 * me_q + d, pl.ds(rows * k, rows)])
    chain_send(0)
    for d in (1, 2, 3):
        copy(block(me_q), block(me_q), y_s.at[d - 1], y_r.at[d - 1], y_to[d]).start()
    copy(block(me_q), block(me_q), c_s.at[0], c_r.at[0]).start()
    x_send(me_t)

    copy(part, sibpart, sib_s, sib_r).wait()
    mine = part[...] + sibpart[...]
    for k in range(16):
        half[k] = mine[4 * k : 4 * k + 4]

    def small(stage, sources, dst, slot, peers):
        for src, to in zip(sources, peers, strict=True):
            copy(src, dst.at[slot], small_s.at[stage], small_r.at[stage], to).start()

    def small_copy(stage, buf):
        return copy(buf.at[pl.ds(0, 15)], buf.at[pl.ds(0, 15)], small_s.at[stage], small_r.at[stage])

    def sum16(buf):
        piece = buf[0]
        for k in range(1, 16):
            piece = piece + buf[k]
        return piece

    small(0, [half.at[px * NY + py] for px, py in plane_peers], rs, plane, plane_to)
    rs[plane] = half[plane]

    mask = jnp.where(iota((8, 128), 1) // 16 == iota((8, 128), 0), 1.0 / 16, 0.0)

    def form(b):
        for u in range(4):
            hb, at = 2 * b + u // 2, (u % 2) * UNIT
            second = tbuf[hb, at + 128 : at + 256, :]
            rolled = pltpu.roll(second.astype(F32), 64, 1).astype(BF16)
            outs = []
            for g in range(2):
                lhs = expand(tbuf[hb, at + 64 * g : at + 64 * g + 64, :].astype(F32), mask).astype(BF16)
                outs.append(mm(lhs, spread(second, rolled, g)))
            store_rows(grads, pl.multiple_of(b * 64 + u * 16, 16), outs)

    @pl.loop(1, 8)
    def _(s):
        chain_recv(s)
        chain_send(s)
        for k in range(CHUNKS):
            for d in range(2):
                ring_send(d, s, k, ring_recv(d, s - 1, k))
        up, down = chain_units(s)
        pl.when(zlo >= s)(lambda: x_send(up))
        pl.when(zlo + s <= ZLO - 1)(lambda: x_send(down))

        @pl.when(s == 1)
        def _():
            small_copy(0, rs).wait_recv()
            zs[z] = sum16(rs)
            small(1, [zs.at[z]] * 15, zs, z, z_to)

        @pl.when(s == 4)
        def _():
            small_copy(1, zs).wait_recv()
            ag[plane] = sum16(zs)
            small(2, [ag.at[plane]] * 15, ag, plane, plane_to)

        e = s - 1

        @pl.when((e >= 1) & (e <= 3))
        def _():
            copy(block(near(e)), block(near(e)), y_s.at[e - 1], y_r.at[e - 1]).wait_recv()
            copy(block(near(e)), block(near(e)), c_s.at[e], c_r.at[e]).start()

        @pl.when(e >= 4)
        def _():
            copy(block(near(e)), block(near(e)), c_s.at[e - 4], c_r.at[e - 4]).wait_recv()

        form(near(e))

        @pl.when(s == 6)
        def _():
            small_copy(2, ag).wait_recv()
            for k in range(16):
                total[4 * k : 4 * k + 4] = ag[k]
            mat, guess = damp(total[...], tokens)
            damped[...] = mat
            inv[...] = newton(mat, guess, 0, 3)

        @pl.when(s == 7)
        def _():
            inv[...] = newton(damped[...], inv[...], 3, 6)

    far_b = far(0)
    for k in range(CHUNKS):
        for d in range(2):
            ring_recv(d, 7, k)
    for d in (1, 2, 3):
        copy(block(far_b), block(far_b), fy_s.at[d - 1], fy_r.at[d - 1], y_to[d]).start()
    copy(block(far_b), block(far_b), c_s.at[4], c_r.at[4]).start()

    inverse = newton(damped[...], inv[...], 6, NEWTON)
    copy(block(near(7)), block(near(7)), c_s.at[3], c_r.at[3]).wait_recv()

    top, bottom = inverse[:64], inverse[64:]
    in_h, in_l = split2(jnp.concatenate([top, pltpu.roll(top, 64, 1)], axis=0))
    out_h, out_l = split2(jnp.concatenate([pltpu.roll(bottom, 64, 1), bottom], axis=0))

    for d in (1, 2, 3):
        src = qbuf.at[pl.ds(lax.rem(x + NX - d, NX) * ZLO, ZLO)]
        copy(src, src, x_s.at[d - 1], x_r.at[d - 1]).wait_recv()

    @pl.loop(0, 32, unroll=4)
    def _(b):
        first = qbuf[b, 0:128, :]
        second = qbuf[b, 128:256, :]
        ppre[b, 0:128, :] = mm(in_h, first) + mm(in_l, first)
        ppre[b, 128:256, :] = mm(second, out_h) + mm(second, out_l)

    def form_query(b):
        second = ppre[b, 128:256, :]
        rolled = pltpu.roll(second, 64, 1)
        outs = []
        for g in range(2):
            lhs = expand(ppre[b, 64 * g : 64 * g + 64, :], mask)
            lhs_h, lhs_l = split2(lhs)
            rhs_h, rhs_l = split2(spread(second, rolled, g))
            both = mm(lhs_h, jnp.concatenate([rhs_h, rhs_l], axis=1))
            outs.append(both[:, :128] + both[:, 128:] + mm(lhs_l, rhs_h))
        store_rows(pre, pl.multiple_of(b * 16, 16), outs)

    @pl.loop(0, 8)
    def _(i):
        for u in range(4):
            form_query(4 * i + u)
        e = i - 3

        @pl.when((e >= 1) & (e <= 3))
        def _():
            copy(block(far(e)), block(far(e)), fy_s.at[e - 1], fy_r.at[e - 1]).wait_recv()
            copy(block(far(e)), block(far(e)), c_s.at[4 + e], c_r.at[4 + e]).start()

    def product(h):
        @pl.loop(0, 4)
        def _(i):
            at = pl.multiple_of(h * 512 + (i // 2) * 256, 256)
            to = pl.multiple_of((i % 2) * 256, 256)
            tile = lax.dot_general(
                grads[pl.ds(at, 256), :], pre[pl.ds(to, 256), :], (((1,), (1,)), ((), ())),
                preferred_element_type=F32,
            )
            out_ref[pl.ds(at, 256), pl.ds(to, 256)] = tile * 0.125

    form(near(7))
    product(zhi)

    @pl.loop(0, 8)
    def _(e):
        @pl.when(e >= 4)
        def _():
            copy(block(far(e)), block(far(e)), c_s.at[e], c_r.at[e]).wait_recv()

        form(far(e))

    product(1 - zhi)

    for d in (1, 2, 3):
        units = qbuf.at[pl.ds(0, ZLO)]
        copy(units, units, x_s.at[d - 1], x_r.at[d - 1]).wait_send()
        copy(block(0), block(0), y_s.at[d - 1], y_r.at[d - 1]).wait_send()
        copy(block(0), block(0), fy_s.at[d - 1], fy_r.at[d - 1]).wait_send()
    for stage, buf in ((0, rs), (1, zs), (2, ag)):
        small_copy(stage, buf).wait_send()

    @pl.loop(0, 8)
    def _(s):
        copy(block(0), block(0), c_s.at[s], c_r.at[s]).wait_send()
        for d in range(2):
            for k in range(CHUNKS):
                i = ring_index(d, s) + k
                slot = tbuf.at[0, pl.ds(0, rows)]
                copy(slot, slot, ring_s.at[i], ring_r.at[i]).wait_send()

        @pl.when((zlo >= s) & (zlo < ZLO - 1))
        def _():
            copy(qbuf.at[0], qbuf.at[0], ku_s.at[s], ku_r.at[s]).wait_send()

        @pl.when((zlo + s <= ZLO - 1) & (zlo > 0))
        def _():
            copy(qbuf.at[0], qbuf.at[0], kd_s.at[s], kd_r.at[s]).wait_send()


def body(train_factors, query_factors):
    tokens = train_factors.shape[0] * train_factors.shape[1] * 512
    train = train_factors.reshape(-1, 128)
    query = query_factors.reshape(-1, 128)
    hbm = pl.BlockSpec(memory_space=pl.ANY)
    dma = pltpu.SemaphoreType.DMA
    return pl.pallas_call(
        functools.partial(kernel, tokens),
        out_shape=jax.ShapeDtypeStruct((1024, 512), F32),
        in_specs=[hbm, hbm],
        out_specs=pl.BlockSpec(memory_space=pltpu.VMEM),
        scratch_shapes=[
            pltpu.VMEM((1024, 128), BF16),
            pltpu.VMEM((256, 128), BF16),
            pltpu.VMEM((STAGE + 14, HALF, 128), BF16),
            pltpu.VMEM((32, UNIT, 128), BF16),
            pltpu.VMEM((1024, 4096), BF16),
            pltpu.VMEM((512, 4096), BF16),
            pltpu.VMEM((32, UNIT, 128), F32),
            pltpu.VMEM((64, 128), F32),
            pltpu.VMEM((64, 128), F32),
            pltpu.VMEM((16, 4, 128), F32),
            pltpu.VMEM((16, 4, 128), F32),
            pltpu.VMEM((16, 4, 128), F32),
            pltpu.VMEM((16, 4, 128), F32),
            pltpu.VMEM((64, 128), F32),
            pltpu.VMEM((128, 128), F32),
            pltpu.VMEM((128, 128), F32),
            dma((2,)), dma, dma, dma((3,)), dma((3,)), dma((16 * CHUNKS,)), dma((16 * CHUNKS,)),
            dma((8,)), dma((8,)), dma((8,)), dma((8,)), dma((3,)), dma((3,)), dma((3,)), dma((3,)), dma((3,)), dma((3,)),
            dma((8,)), dma((8,)),
        ],
        compiler_params=pltpu.CompilerParams(
            collective_id=0, has_side_effects=True, vmem_limit_bytes=48 * 2**20
        ),
        name="influence",
    )(train, query)


def solution(mesh):
    return jax.shard_map(
        body,
        mesh=mesh,
        in_specs=(P(("train", "query"), None, None), P(("query", "train"), None, None)),
        out_specs=P("train", "query"),
        check_vma=False,
    )
```

```python
import functools

import jax
import jax.numpy as jnp
from jax import lax
from jax.experimental import pallas as pl
from jax.experimental.pallas import tpu as pltpu
from jax.sharding import PartitionSpec as P

MESH = pl.DeviceIdType.MESH
F32 = jnp.float32
BF16 = jnp.bfloat16

NX, NY, NZ, ZLO = 4, 4, 16, 8
UNIT = 256
HALF = 512
STAGE = 32
CHUNKS = 2
STOPS = 8
NEWTON = 8
LOW, HIGH = 0.1, 64.1


def coordinates():
    t = lax.axis_index("train")
    q = lax.axis_index("query")
    return t // ZLO, (q // 2) % NY, (q // (2 * NY)) * ZLO + t % ZLO, q % 2


def device(x, y, z, c):
    return (x * ZLO + z % ZLO, (z // ZLO) * (2 * NY) + y * 2 + c)


def iota(shape, dim):
    return lax.broadcasted_iota(jnp.int32, shape, dim)


def split2(v):
    hi = v.astype(BF16)
    return hi, (v - hi.astype(F32)).astype(BF16)


def mm(a, b):
    return jnp.dot(a, b, preferred_element_type=F32)


def mm3(a, b):
    ah, al = split2(a)
    bh, bl = split2(b)
    return mm(ah, bh) + (mm(ah, bl) + mm(al, bh))


def mmh(a, b):
    return jnp.dot(a, b, preferred_element_type=F32, precision=lax.Precision.HIGHEST)


def eye128():
    return jnp.where(iota((128, 128), 0) == iota((128, 128), 1), 1.0, 0.0)


def damp(total, tokens):
    row, lane = iota((64, 128), 0), iota((64, 128), 1)
    cov = total * (1.0 / tokens)
    first = lane < 64
    tr_in = jnp.sum(jnp.where(lane == row, cov, 0.0)) * (1.0 / 64)
    tr_out = jnp.sum(jnp.where(lane == row + 64, cov, 0.0)) * (1.0 / 64)
    top = jnp.where(first, cov + jnp.where(lane == row, 0.1 * tr_in, 0.0), 0.0)
    bottom = jnp.where(first, 0.0, cov + jnp.where(lane == row + 64, 0.1 * tr_out, 0.0))
    r, lanes = iota((128, 128), 0), iota((128, 128), 1)
    mean = jnp.where(r < 64, tr_in, tr_out)
    guess = jnp.where(r == lanes, (2.0 / (LOW + HIGH)) / mean, 0.0)
    return jnp.concatenate([top, bottom], axis=0), guess


def newton(damped, inv, lo, hi):
    bound = 2.0 * LOW / (LOW + HIGH)
    for step in range(hi):
        mapped = bound * (2.0 - bound)
        plain = step >= NEWTON - 2
        if step >= lo:
            mul = mmh if plain else mm3
            inv = mul(inv, 2.0 * eye128() - mul(damped, inv))
            if not plain:
                inv = inv * (2.0 / (1.0 + mapped))
        bound = 2.0 * mapped / (1.0 + mapped)
    return inv


def expand(first_t, mask):
    rows = []
    for i in range(32):
        a = jnp.broadcast_to(first_t[i : i + 1], (8, 128)) * mask
        b = jnp.broadcast_to(first_t[32 + i : 33 + i], (8, 128)) * mask
        rows.append(jnp.concatenate([a, b], axis=1))
    return jnp.concatenate(rows, axis=0)


def spread(second, rolled, group):
    left = iota((128, 128), 1) < 64
    zero = jnp.zeros_like(second)
    if group == 0:
        return jnp.concatenate([jnp.where(left, second, zero), jnp.where(left, zero, rolled)], axis=0)
    return jnp.concatenate([jnp.where(left, rolled, zero), jnp.where(left, zero, second)], axis=0)


def store_rows(out_ref, row, pair):
    a, b = pair
    for i in range(32):
        tile = jnp.concatenate([a[8 * i : 8 * i + 8], b[8 * i : 8 * i + 8]], axis=0)
        out_ref[pl.ds(row, 16), 128 * i : 128 * i + 128] = tile.astype(BF16)


def kernel(
    tokens, train_hbm, query_hbm, out_ref, train_ref, query_ref, tbuf, qbuf, grads, pre, part, sibpart, half, rs, zs,
    ag, total, weights, in_sem, sib_s, sib_r, small_s, small_r, ring_s, ring_r, ku_s, ku_r, kd_s, kd_r, x_s, x_r,
    y_s, y_r, fy_s, fy_r, g_s, g_r,
):
    x, y, z, c = coordinates()
    me_t = lax.axis_index("train")
    me_q = lax.axis_index("query")
    plane = x * NY + y
    sibling = device(x, y, z, 1 - c)
    zlo = lax.rem(z, ZLO)
    zhi = z // ZLO
    plane_peers = [
        (lax.rem(x + dx, NX), lax.rem(y + dy, NY)) for dx in range(NX) for dy in range(NY) if dx or dy
    ]
    plane_to = [device(px, py, z, c) for px, py in plane_peers]
    z_to = [device(x, y, lax.rem(z + dz, NZ), c) for dz in range(1, NZ)]
    x_to = [device(lax.rem(x + d, NX), y, z, c) for d in range(NX)]
    y_to = [device(x, lax.rem(y + d, NY), z, c) for d in range(NY)]

    inputs = [
        pltpu.make_async_copy(train_hbm, train_ref, in_sem.at[0]),
        pltpu.make_async_copy(query_hbm, query_ref, in_sem.at[1]),
    ]
    for cp in inputs:
        cp.start()
    barrier = pltpu.get_barrier_semaphore()
    for to in [*z_to, *plane_to, sibling]:
        pl.semaphore_signal(barrier, inc=1, device_id=to, device_id_type=MESH)
    for cp in inputs:
        cp.wait()

    left = iota((128, 128), 1) < 64

    def arrange(src, at, dst, block, to):
        a = src[pl.ds(at, 128), :]
        b = src[pl.ds(at + 128, 128), :]
        a32, b32 = a.astype(F32), b.astype(F32)
        at32, bt32 = a32.T, b32.T
        dst[block, pl.ds(to, 64), :] = at32[:64].astype(BF16)
        dst[block, pl.ds(to + 64, 64), :] = bt32[:64].astype(BF16)
        dst[block, pl.ds(to + 128, 128), :] = jnp.where(left, pltpu.roll(a32, 64, 1), b32).astype(BF16)
        return a, b, at32.astype(BF16), bt32.astype(BF16)

    cov = jnp.zeros((128, 128), F32)
    for u in range(4):
        a, b, at, bt = arrange(train_ref, u * UNIT, tbuf, 2 * me_q + u // 2, (u % 2) * UNIT)
        cov = cov + mm(at, a) + mm(bt, b)
    arrange(query_ref, 0, qbuf, me_t, 0)
    part[...] = jnp.where(iota((64, 128), 1) < 64, cov[:64], cov[64:])

    pl.semaphore_wait(barrier, 31)

    def copy(src, dst, ssem, rsem, to=sibling):
        return pltpu.make_async_remote_copy(
            src_ref=src, dst_ref=dst, send_sem=ssem, recv_sem=rsem, device_id=to, device_id_type=MESH
        )

    rows = HALF // CHUNKS

    def ring_index(d, step):
        return (step * 2 + d) * CHUNKS

    def ring_slot(d, step, k):
        landed = 2 * lax.rem(me_q + 8, 16) + d
        return tbuf.at[jnp.where(step < STOPS - 1, STAGE + d * 7 + step, landed), pl.ds(rows * k, rows)]

    def ring_send(d, step, k, src):
        zr = lax.rem(z + (1 if d == 0 else NZ - 1), NZ)
        landed = 2 * ((1 - zr // ZLO) * 8 + 2 * y + c) + d
        dst = tbuf.at[jnp.where(step < STOPS - 1, STAGE + d * 7 + step, landed), pl.ds(rows * k, rows)]
        i = ring_index(d, step) + k
        copy(src, dst, ring_s.at[i], ring_r.at[i], device(x, y, zr, c)).start()

    def ring_recv(d, step, k):
        i = ring_index(d, step) + k
        slot = ring_slot(d, step, k)
        copy(slot, slot, ring_s.at[i], ring_r.at[i]).wait_recv()
        return slot

    def chain_units(s):
        return me_t - jnp.minimum(s, zlo), me_t + jnp.minimum(s, ZLO - 1 - zlo)

    def chain_send(s):
        up, down = chain_units(s)

        @pl.when((zlo >= s) & (zlo < ZLO - 1))
        def _():
            to = device(x, y, jnp.minimum(z + 1, NZ - 1), c)
            copy(qbuf.at[up], qbuf.at[up], ku_s.at[s], ku_r.at[s], to).start()

        @pl.when((zlo + s <= ZLO - 1) & (zlo > 0))
        def _():
            to = device(x, y, jnp.maximum(z - 1, 0), c)
            copy(qbuf.at[down], qbuf.at[down], kd_s.at[s], kd_r.at[s], to).start()

    def chain_recv(s):
        up, down = chain_units(s)

        @pl.when(zlo >= s)
        def _():
            copy(qbuf.at[up], qbuf.at[up], ku_s.at[s - 1], ku_r.at[s - 1]).wait_recv()

        @pl.when(zlo + s <= ZLO - 1)
        def _():
            copy(qbuf.at[down], qbuf.at[down], kd_s.at[s - 1], kd_r.at[s - 1]).wait_recv()

    def x_send(unit, j):
        for d in (1, 2, 3):
            copy(qbuf.at[unit], qbuf.at[unit], x_s.at[d - 1], x_r.at[16 * (d - 1) + j], x_to[d]).start()

    def block(b):
        return tbuf.at[pl.ds(2 * b, 2)]

    def near(e):
        other = e // 4
        return me_q - lax.rem(me_q, 8) + 2 * lax.rem(y + NY - lax.rem(e, 4), NY) + (c + other - 2 * c * other)

    def far(e):
        return lax.rem(near(e) + 8, 16)

    copy(part, sibpart, sib_s, sib_r).start()
    for k in range(CHUNKS):
        for d in range(2):
            ring_send(d, 0, k, tbuf.at[2 * me_q + d, pl.ds(rows * k, rows)])
    chain_send(0)
    for d in (1, 2, 3):
        copy(block(me_q), block(me_q), y_s.at[d - 1], y_r.at[d - 1], y_to[d]).start()
    x_send(me_t, 0)

    copy(part, sibpart, sib_s, sib_r).wait()
    mine = part[...] + sibpart[...]
    for k in range(16):
        half[k] = mine[4 * k : 4 * k + 4]

    def small(stage, sources, dst, slot, peers):
        for src, to in zip(sources, peers, strict=True):
            copy(src, dst.at[slot], small_s.at[stage], small_r.at[stage], to).start()

    def small_copy(stage, buf):
        return copy(buf.at[pl.ds(0, 15)], buf.at[pl.ds(0, 15)], small_s.at[stage], small_r.at[stage])

    def sum16(buf):
        piece = buf[0]
        for k in range(1, 16):
            piece = piece + buf[k]
        return piece

    small(0, [half.at[px * NY + py] for px, py in plane_peers], rs, plane, plane_to)
    rs[plane] = half[plane]

    mask = jnp.where(iota((8, 128), 1) // 16 == iota((8, 128), 0), 1.0 / 16, 0.0)

    def form_half(hb, row):
        for u in range(2):
            second = tbuf[hb, u * UNIT + 128 : u * UNIT + 256, :]
            rolled = pltpu.roll(second.astype(F32), 64, 1).astype(BF16)
            outs = []
            for g in range(2):
                first = tbuf[hb, u * UNIT + 64 * g : u * UNIT + 64 * g + 64, :]
                lhs = expand(first.astype(F32), mask).astype(BF16)
                outs.append(mm(lhs, spread(second, rolled, g)))
            store_rows(grads, pl.multiple_of(row + u * 16, 16), outs)

    def form(b, row):
        form_half(2 * b, row)
        form_half(2 * b + 1, row + 32)

    def grad_copy(row, i):
        rows_of = grads.at[pl.ds(pl.multiple_of(row, 64), 64)]
        return copy(rows_of, rows_of, g_s.at[i], g_r.at[i])

    far_rows = (1 - zhi) * 512
    far_y = [y, lax.rem(y + 3, NY), lax.rem(y + 1, NY), lax.rem(y + 2, NY)]

    def query_units(units):
        firsts, seconds = [], []
        for b in units:
            first = qbuf[b, 0:128, :]
            second = qbuf[b, 128:256, :]
            firsts.append(mm(weights[0], first) + mm(weights[1], first))
            seconds.append(mm(second, weights[2]) + mm(second, weights[3]))
        for b, first_p, second_p in zip(units, firsts, seconds, strict=True):
            rolled = pltpu.roll(second_p, 64, 1)
            outs = []
            for g in range(2):
                lhs_h, lhs_l = split2(expand(first_p[64 * g : 64 * g + 64], mask))
                rhs_h, rhs_l = split2(spread(second_p, rolled, g))
                both = mm(lhs_h, jnp.concatenate([rhs_h, rhs_l], axis=1))
                outs.append(both[:, :128] + both[:, 128:] + mm(lhs_l, rhs_h))
            store_rows(pre, pl.multiple_of(b * 16, 16), outs)

    def query_batch(j):
        far_z = j // 2
        above = j % 2 == 1
        shift = jnp.where(above, far_z, -far_z)

        @pl.when((above & (far_z > 0) & (zlo + far_z <= ZLO - 1)) | (jnp.logical_not(above) & (zlo >= far_z)))
        def _():
            units = [lax.rem(x + NX - d, NX) * ZLO + zlo + shift for d in range(NX)]
            for d in (1, 2, 3):
                b = qbuf.at[units[d]]
                copy(b, b, x_s.at[d - 1], x_r.at[16 * (d - 1) + j]).wait_recv()
            query_units(units)

    def far_half(e, d):
        return tbuf.at[2 * far(e) + d]

    def fy(e, d, i, to=0):
        return copy(far_half(e, d), far_half(e, d), fy_s.at[i], fy_r.at[i], y_to[to])

    def land():
        for d in range(2):
            for k in range(CHUNKS):
                ring_recv(d, STOPS - 1, k)
            fy(0, d, d, 1 if d == 0 else 3).start()
        fy(0, 1, 2, 1).start()
        fy(0, 0, 3, 3).start()

    def pass_on():
        fy(1, 0, 0).wait_recv()
        fy(1, 0, 4, 1).start()
        fy(3, 1, 1).wait_recv()
        fy(3, 1, 5, 3).start()

    @pl.loop(1, 9)
    def _(s):
        chain_recv(s)
        chain_send(s)

        @pl.when(s < STOPS)
        def _():
            for k in range(CHUNKS):
                for d in range(2):
                    ring_send(d, s, k, ring_recv(d, s - 1, k))

        up, down = chain_units(s)
        pl.when(zlo >= s)(lambda: x_send(up, 2 * s))
        pl.when(zlo + s <= ZLO - 1)(lambda: x_send(down, 2 * s + 1))

        @pl.when(s == 2)
        def _():
            small_copy(0, rs).wait_recv()
            zs[z] = sum16(rs)
            small(1, [zs.at[z]] * 15, zs, z, z_to)

        @pl.when(s == 4)
        def _():
            small_copy(1, zs).wait_recv()
            ag[plane] = sum16(zs)
            small(2, [ag.at[plane]] * 15, ag, plane, plane_to)

        e = s - 1

        @pl.when((e >= 1) & (e <= 3))
        def _():
            copy(block(near(e)), block(near(e)), y_s.at[e - 1], y_r.at[e - 1]).wait_recv()

        @pl.when(e <= 3)
        def _():
            form(near(e), 64 * near(e))
            grad_copy(64 * near(e), e).start()

        @pl.when(s == 5)
        def _():
            small_copy(2, ag).wait_recv()
            for k in range(16):
                total[4 * k : 4 * k + 4] = ag[k]
            mat, guess = damp(total[...], tokens)
            inverse = newton(mat, guess, 0, NEWTON)
            top, bottom = inverse[:64], inverse[64:]
            weights[0], weights[1] = split2(jnp.concatenate([top, pltpu.roll(top, 64, 1)], axis=0))
            weights[2], weights[3] = split2(jnp.concatenate([pltpu.roll(bottom, 64, 1), bottom], axis=0))

        pl.when(s == STOPS)(land)

        @pl.loop(jnp.where(s <= 6, 0, 4 * (s - 6)), jnp.where(s <= 5, 0, jnp.where(s == 8, 16, 4 * (s - 5))))
        def _(j):
            query_batch(j)

        pl.when(s == STOPS)(pass_on)

    for e in range(4):
        grad_copy(0, e).wait_recv()

    @pl.loop(0, 2)
    def _(i):
        at = pl.multiple_of(zhi * 512, 512)
        to = pl.multiple_of(i * 256, 256)
        tile = lax.dot_general(
            grads[pl.ds(at, 512), :], pre[pl.ds(to, 256), :], (((1,), (1,)), ((), ())), preferred_element_type=F32
        )
        out_ref[pl.ds(at, 512), pl.ds(to, 256)] = tile * 0.125

    @pl.loop(0, 4)
    def _(i):
        e = jnp.where(i == 2, 3, jnp.where(i == 3, 2, i))

        @pl.when(i == 1)
        def _():
            fy(1, 1, 2).wait_recv()

        @pl.when(i == 2)
        def _():
            fy(3, 0, 3).wait_recv()

        @pl.when(i == 3)
        def _():
            fy(2, 0, 4).wait_recv()
            fy(2, 1, 5).wait_recv()

        row = far_rows + 128 * i + 64 * c
        form(far(e), row)
        grad_copy(row, 4 + i).start()

    @pl.loop(0, 2)
    def _(i):
        grad_copy(0, 4 + 2 * i).wait_recv()
        grad_copy(0, 5 + 2 * i).wait_recv()
        at = pl.multiple_of(far_rows + 256 * i, 256)
        tile = lax.dot_general(
            grads[pl.ds(at, 256), :], pre[...], (((1,), (1,)), ((), ())), preferred_element_type=F32
        )
        for k in range(2):
            to = far_rows + 128 * jnp.where(i == 0, far_y[k], far_y[2 + k])
            out_ref[pl.ds(pl.multiple_of(to, 128), 128), :] = tile[128 * k : 128 * k + 128] * 0.125

    for d in (1, 2, 3):
        units = qbuf.at[pl.ds(0, ZLO)]
        copy(units, units, x_s.at[d - 1], x_r.at[d - 1]).wait_send()
        copy(block(0), block(0), y_s.at[d - 1], y_r.at[d - 1]).wait_send()
    for i in range(6):
        fy(0, 0, i).wait_send()
    for stage, buf in ((0, rs), (1, zs), (2, ag)):
        small_copy(stage, buf).wait_send()

    @pl.loop(0, 8)
    def _(s):
        grad_copy(0, s).wait_send()

        @pl.when(s < STOPS)
        def _():
            for d in range(2):
                for k in range(CHUNKS):
                    i = ring_index(d, s) + k
                    slot = tbuf.at[0, pl.ds(0, rows)]
                    copy(slot, slot, ring_s.at[i], ring_r.at[i]).wait_send()

        @pl.when((zlo >= s) & (zlo < ZLO - 1))
        def _():
            copy(qbuf.at[0], qbuf.at[0], ku_s.at[s], ku_r.at[s]).wait_send()

        @pl.when((zlo + s <= ZLO - 1) & (zlo > 0))
        def _():
            copy(qbuf.at[0], qbuf.at[0], kd_s.at[s], kd_r.at[s]).wait_send()


def body(train_factors, query_factors):
    tokens = train_factors.shape[0] * train_factors.shape[1] * 512
    train = train_factors.reshape(-1, 128)
    query = query_factors.reshape(-1, 128)
    hbm = pl.BlockSpec(memory_space=pltpu.HBM)
    dma = pltpu.SemaphoreType.DMA
    return pl.pallas_call(
        functools.partial(kernel, tokens),
        out_shape=jax.ShapeDtypeStruct((1024, 512), F32),
        in_specs=[hbm, hbm],
        out_specs=pl.BlockSpec(memory_space=pltpu.VMEM),
        scratch_shapes=[
            pltpu.VMEM((1024, 128), BF16),
            pltpu.VMEM((256, 128), BF16),
            pltpu.VMEM((STAGE + 14, HALF, 128), BF16),
            pltpu.VMEM((32, UNIT, 128), BF16),
            pltpu.VMEM((1024, 4096), BF16),
            pltpu.VMEM((512, 4096), BF16),
            pltpu.VMEM((64, 128), F32),
            pltpu.VMEM((64, 128), F32),
            pltpu.VMEM((16, 4, 128), F32),
            pltpu.VMEM((16, 4, 128), F32),
            pltpu.VMEM((16, 4, 128), F32),
            pltpu.VMEM((16, 4, 128), F32),
            pltpu.VMEM((64, 128), F32),
            pltpu.VMEM((4, 128, 128), BF16),
            dma((2,)), dma, dma, dma((3,)), dma((3,)), dma((16 * CHUNKS,)), dma((16 * CHUNKS,)),
            dma((9,)), dma((9,)), dma((9,)), dma((9,)), dma((3,)), dma((48,)), dma((3,)), dma((3,)), dma((6,)), dma((6,)),
            dma((8,)), dma((8,)),
        ],
        compiler_params=pltpu.CompilerParams(
            collective_id=0, has_side_effects=True, vmem_limit_bytes=63 * 2**20
        ),
        name="influence",
    )(train, query)


def solution(mesh):
    return jax.shard_map(
        body,
        mesh=mesh,
        in_specs=(P(("train", "query"), None, None), P(("query", "train"), None, None)),
        out_specs=P("train", "query"),
        check_vma=False,
    )
```

```python
import functools

import jax
import jax.numpy as jnp
from jax import lax
from jax.experimental import pallas as pl
from jax.experimental.pallas import tpu as pltpu
from jax.sharding import PartitionSpec as P

MESH = pl.DeviceIdType.MESH
F32 = jnp.float32
BF16 = jnp.bfloat16

NX, NY, NZ, ZLO = 4, 4, 16, 8
UNIT = 256
HALF = 512
STAGE = 32
CHUNKS = 2
STOPS = 8
NEWTON = 8
LOW, HIGH = 0.1, 64.1


def coordinates():
    t = lax.axis_index("train")
    q = lax.axis_index("query")
    return t // ZLO, (q // 2) % NY, (q // (2 * NY)) * ZLO + t % ZLO, q % 2


def device(x, y, z, c):
    return (x * ZLO + z % ZLO, (z // ZLO) * (2 * NY) + y * 2 + c)


def iota(shape, dim):
    return lax.broadcasted_iota(jnp.int32, shape, dim)


def split2(v):
    hi = v.astype(BF16)
    return hi, (v - hi.astype(F32)).astype(BF16)


def mm(a, b):
    return jnp.dot(a, b, preferred_element_type=F32)


def mm3(a, b):
    ah, al = split2(a)
    bh, bl = split2(b)
    return mm(ah, bh) + (mm(ah, bl) + mm(al, bh))


def mmh(a, b):
    return jnp.dot(a, b, preferred_element_type=F32, precision=lax.Precision.HIGHEST)


def eye128():
    return jnp.where(iota((128, 128), 0) == iota((128, 128), 1), 1.0, 0.0)


def damp(total, tokens):
    row, lane = iota((64, 128), 0), iota((64, 128), 1)
    cov = total * (1.0 / tokens)
    first = lane < 64
    tr_in = jnp.sum(jnp.where(lane == row, cov, 0.0)) * (1.0 / 64)
    tr_out = jnp.sum(jnp.where(lane == row + 64, cov, 0.0)) * (1.0 / 64)
    top = jnp.where(first, cov + jnp.where(lane == row, 0.1 * tr_in, 0.0), 0.0)
    bottom = jnp.where(first, 0.0, cov + jnp.where(lane == row + 64, 0.1 * tr_out, 0.0))
    r, lanes = iota((128, 128), 0), iota((128, 128), 1)
    mean = jnp.where(r < 64, tr_in, tr_out)
    guess = jnp.where(r == lanes, (2.0 / (LOW + HIGH)) / mean, 0.0)
    return jnp.concatenate([top, bottom], axis=0), guess


def newton(damped, inv, lo, hi):
    bound = 2.0 * LOW / (LOW + HIGH)
    for step in range(hi):
        mapped = bound * (2.0 - bound)
        plain = step >= NEWTON - 2
        if step >= lo:
            mul = mmh if plain else mm3
            inv = mul(inv, 2.0 * eye128() - mul(damped, inv))
            if not plain:
                inv = inv * (2.0 / (1.0 + mapped))
        bound = 2.0 * mapped / (1.0 + mapped)
    return inv


def expand(first_t, mask):
    rows = []
    for i in range(32):
        a = jnp.broadcast_to(first_t[i : i + 1], (8, 128)) * mask
        b = jnp.broadcast_to(first_t[32 + i : 33 + i], (8, 128)) * mask
        rows.append(jnp.concatenate([a, b], axis=1))
    return jnp.concatenate(rows, axis=0)


def spread(second, rolled, group):
    left = iota((128, 128), 1) < 64
    zero = jnp.zeros_like(second)
    if group == 0:
        return jnp.concatenate([jnp.where(left, second, zero), jnp.where(left, zero, rolled)], axis=0)
    return jnp.concatenate([jnp.where(left, rolled, zero), jnp.where(left, zero, second)], axis=0)


def store_rows(out_ref, row, pair):
    a, b = pair
    for i in range(32):
        tile = jnp.concatenate([a[8 * i : 8 * i + 8], b[8 * i : 8 * i + 8]], axis=0)
        out_ref[pl.ds(row, 16), 128 * i : 128 * i + 128] = tile.astype(BF16)


def kernel(
    tokens, train_hbm, query_hbm, out_ref, train_ref, query_ref, tbuf, qbuf, grads, pre, part, sibpart, half, rs, zs,
    ag, total, weights, in_sem, sib_s, sib_r, small_s, small_r, ring_s, ring_r, ku_s, ku_r, kd_s, kd_r, x_s, x_r,
    y_s, y_r, fy_s, fy_r, g_s, g_r,
):
    x, y, z, c = coordinates()
    me_t = lax.axis_index("train")
    me_q = lax.axis_index("query")
    plane = x * NY + y
    sibling = device(x, y, z, 1 - c)
    zlo = lax.rem(z, ZLO)
    zhi = z // ZLO
    plane_peers = [
        (lax.rem(x + dx, NX), lax.rem(y + dy, NY)) for dx in range(NX) for dy in range(NY) if dx or dy
    ]
    plane_to = [device(px, py, z, c) for px, py in plane_peers]
    z_to = [device(x, y, lax.rem(z + dz, NZ), c) for dz in range(1, NZ)]
    x_to = [device(lax.rem(x + d, NX), y, z, c) for d in range(NX)]
    y_to = [device(x, lax.rem(y + d, NY), z, c) for d in range(NY)]

    inputs = [
        pltpu.make_async_copy(train_hbm, train_ref, in_sem.at[0]),
        pltpu.make_async_copy(query_hbm, query_ref, in_sem.at[1]),
    ]
    for cp in inputs:
        cp.start()
    barrier = pltpu.get_barrier_semaphore()
    for to in [*z_to, *plane_to, sibling]:
        pl.semaphore_signal(barrier, inc=1, device_id=to, device_id_type=MESH)
    for cp in inputs:
        cp.wait()

    left = iota((128, 128), 1) < 64

    def arrange(src, at, dst, block, to):
        a = src[pl.ds(at, 128), :]
        b = src[pl.ds(at + 128, 128), :]
        a32, b32 = a.astype(F32), b.astype(F32)
        at32, bt32 = a32.T, b32.T
        dst[block, pl.ds(to, 64), :] = at32[:64].astype(BF16)
        dst[block, pl.ds(to + 64, 64), :] = bt32[:64].astype(BF16)
        dst[block, pl.ds(to + 128, 128), :] = jnp.where(left, pltpu.roll(a32, 64, 1), b32).astype(BF16)
        return a, b, at32.astype(BF16), bt32.astype(BF16)

    cov = jnp.zeros((128, 128), F32)
    for u in range(4):
        a, b, at, bt = arrange(train_ref, u * UNIT, tbuf, 2 * me_q + u // 2, (u % 2) * UNIT)
        cov = cov + mm(at, a) + mm(bt, b)
    arrange(query_ref, 0, qbuf, me_t, 0)
    part[...] = jnp.where(iota((64, 128), 1) < 64, cov[:64], cov[64:])

    pl.semaphore_wait(barrier, 31)

    def copy(src, dst, ssem, rsem, to=sibling):
        return pltpu.make_async_remote_copy(
            src_ref=src, dst_ref=dst, send_sem=ssem, recv_sem=rsem, device_id=to, device_id_type=MESH
        )

    rows = HALF // CHUNKS

    def ring_index(d, step):
        return (step * 2 + d) * CHUNKS

    def ring_slot(d, step, k):
        landed = 2 * lax.rem(me_q + 8, 16) + d
        return tbuf.at[jnp.where(step < STOPS - 1, STAGE + d * 7 + step, landed), pl.ds(rows * k, rows)]

    def ring_send(d, step, k, src):
        zr = lax.rem(z + (1 if d == 0 else NZ - 1), NZ)
        landed = 2 * ((1 - zr // ZLO) * 8 + 2 * y + c) + d
        dst = tbuf.at[jnp.where(step < STOPS - 1, STAGE + d * 7 + step, landed), pl.ds(rows * k, rows)]
        i = ring_index(d, step) + k
        copy(src, dst, ring_s.at[i], ring_r.at[i], device(x, y, zr, c)).start()

    def ring_recv(d, step, k):
        i = ring_index(d, step) + k
        slot = ring_slot(d, step, k)
        copy(slot, slot, ring_s.at[i], ring_r.at[i]).wait_recv()
        return slot

    def chain_units(s):
        return me_t - jnp.minimum(s, zlo), me_t + jnp.minimum(s, ZLO - 1 - zlo)

    def chain_send(s):
        up, down = chain_units(s)

        @pl.when((zlo >= s) & (zlo < ZLO - 1))
        def _():
            to = device(x, y, jnp.minimum(z + 1, NZ - 1), c)
            copy(qbuf.at[up], qbuf.at[up], ku_s.at[s], ku_r.at[s], to).start()

        @pl.when((zlo + s <= ZLO - 1) & (zlo > 0))
        def _():
            to = device(x, y, jnp.maximum(z - 1, 0), c)
            copy(qbuf.at[down], qbuf.at[down], kd_s.at[s], kd_r.at[s], to).start()

    def chain_recv(s):
        up, down = chain_units(s)

        @pl.when(zlo >= s)
        def _():
            copy(qbuf.at[up], qbuf.at[up], ku_s.at[s - 1], ku_r.at[s - 1]).wait_recv()

        @pl.when(zlo + s <= ZLO - 1)
        def _():
            copy(qbuf.at[down], qbuf.at[down], kd_s.at[s - 1], kd_r.at[s - 1]).wait_recv()

    def x_send(unit, j):
        for d in (1, 2, 3):
            copy(qbuf.at[unit], qbuf.at[unit], x_s.at[d - 1], x_r.at[16 * (d - 1) + j], x_to[d]).start()

    def block(b):
        return tbuf.at[pl.ds(2 * b, 2)]

    def near(e):
        other = e // 4
        return me_q - lax.rem(me_q, 8) + 2 * lax.rem(y + NY - lax.rem(e, 4), NY) + (c + other - 2 * c * other)

    def far(e):
        return lax.rem(near(e) + 8, 16)

    copy(part, sibpart, sib_s, sib_r).start()
    for k in range(CHUNKS):
        for d in range(2):
            ring_send(d, 0, k, tbuf.at[2 * me_q + d, pl.ds(rows * k, rows)])
    chain_send(0)
    for d in (1, 2, 3):
        copy(block(me_q), block(me_q), y_s.at[d - 1], y_r.at[d - 1], y_to[d]).start()
    x_send(me_t, 0)

    copy(part, sibpart, sib_s, sib_r).wait()
    mine = part[...] + sibpart[...]
    for k in range(16):
        half[k] = mine[4 * k : 4 * k + 4]

    def small(stage, sources, dst, slot, peers):
        for src, to in zip(sources, peers, strict=True):
            copy(src, dst.at[slot], small_s.at[stage], small_r.at[stage], to).start()

    def small_copy(stage, buf):
        return copy(buf.at[pl.ds(0, 15)], buf.at[pl.ds(0, 15)], small_s.at[stage], small_r.at[stage])

    def sum16(buf):
        piece = buf[0]
        for k in range(1, 16):
            piece = piece + buf[k]
        return piece

    small(0, [half.at[px * NY + py] for px, py in plane_peers], rs, plane, plane_to)
    rs[plane] = half[plane]

    mask = jnp.where(iota((8, 128), 1) // 16 == iota((8, 128), 0), 1.0 / 16, 0.0)

    def form_half(hb, row):
        for u in range(2):
            second = tbuf[hb, u * UNIT + 128 : u * UNIT + 256, :]
            rolled = pltpu.roll(second.astype(F32), 64, 1).astype(BF16)
            outs = []
            for g in range(2):
                first = tbuf[hb, u * UNIT + 64 * g : u * UNIT + 64 * g + 64, :]
                lhs = expand(first.astype(F32), mask).astype(BF16)
                outs.append(mm(lhs, spread(second, rolled, g)))
            store_rows(grads, pl.multiple_of(row + u * 16, 16), outs)

    def form(b, row):
        form_half(2 * b, row)
        form_half(2 * b + 1, row + 32)

    def grad_copy(row, i):
        rows_of = grads.at[pl.ds(pl.multiple_of(row, 64), 64)]
        return copy(rows_of, rows_of, g_s.at[i], g_r.at[i])

    far_rows = (1 - zhi) * 512
    far_y = [y, lax.rem(y + 3, NY), lax.rem(y + 1, NY), lax.rem(y + 2, NY)]

    def query_units(units):
        firsts, seconds = [], []
        for b in units:
            first = qbuf[b, 0:128, :]
            second = qbuf[b, 128:256, :]
            firsts.append(mm(weights[0], first) + mm(weights[1], first))
            seconds.append(mm(second, weights[2]) + mm(second, weights[3]))
        for b, first_p, second_p in zip(units, firsts, seconds, strict=True):
            rolled = pltpu.roll(second_p, 64, 1)
            outs = []
            for g in range(2):
                lhs_h, lhs_l = split2(expand(first_p[64 * g : 64 * g + 64], mask))
                rhs_h, rhs_l = split2(spread(second_p, rolled, g))
                both = mm(lhs_h, jnp.concatenate([rhs_h, rhs_l], axis=1))
                outs.append(both[:, :128] + both[:, 128:] + mm(lhs_l, rhs_h))
            store_rows(pre, pl.multiple_of(b * 16, 16), outs)

    def query_batch(j):
        far_z = j // 2
        above = j % 2 == 1
        shift = jnp.where(above, far_z, -far_z)

        @pl.when((above & (far_z > 0) & (zlo + far_z <= ZLO - 1)) | (jnp.logical_not(above) & (zlo >= far_z)))
        def _():
            units = [lax.rem(x + NX - d, NX) * ZLO + zlo + shift for d in range(NX)]
            for d in (1, 2, 3):
                b = qbuf.at[units[d]]
                copy(b, b, x_s.at[d - 1], x_r.at[16 * (d - 1) + j]).wait_recv()
            query_units(units)

    def far_half(e, d):
        return tbuf.at[2 * far(e) + d]

    def fy(e, d, i, to=0):
        return copy(far_half(e, d), far_half(e, d), fy_s.at[i], fy_r.at[i], y_to[to])

    def fyc(e, d, k, i, to=0):
        part_of = tbuf.at[2 * far(e) + d, pl.ds(rows * k, rows)]
        j = 6 + 2 * i + k
        return copy(part_of, part_of, fy_s.at[j], fy_r.at[j], y_to[to])

    def land():
        for k in range(CHUNKS):
            for d in range(2):
                ring_recv(d, STOPS - 1, k)
                fyc(0, d, k, d, 1 if d == 0 else 3).start()
        fy(0, 1, 2, 1).start()
        fy(0, 0, 3, 3).start()

    def pass_on():
        for k in range(CHUNKS):
            fyc(1, 0, k, 0).wait_recv()
            fyc(1, 0, k, 2, 1).start()
            fyc(3, 1, k, 1).wait_recv()
            fyc(3, 1, k, 3, 3).start()

    @pl.loop(1, 9)
    def _(s):
        @pl.when(s < STOPS)
        def _():
            for k in range(CHUNKS):
                for d in range(2):
                    ring_send(d, s, k, ring_recv(d, s - 1, k))

        chain_recv(s)
        chain_send(s)

        up, down = chain_units(s)
        pl.when(zlo >= s)(lambda: x_send(up, 2 * s))
        pl.when(zlo + s <= ZLO - 1)(lambda: x_send(down, 2 * s + 1))

        @pl.when(s == 2)
        def _():
            small_copy(0, rs).wait_recv()
            zs[z] = sum16(rs)
            small(1, [zs.at[z]] * 15, zs, z, z_to)

        @pl.when(s == 5)
        def _():
            small_copy(1, zs).wait_recv()
            ag[plane] = sum16(zs)
            small(2, [ag.at[plane]] * 15, ag, plane, plane_to)

        e = s - 1

        @pl.when((e >= 1) & (e <= 3))
        def _():
            copy(block(near(e)), block(near(e)), y_s.at[e - 1], y_r.at[e - 1]).wait_recv()

        @pl.when(e <= 3)
        def _():
            form(near(e), 64 * near(e))
            grad_copy(64 * near(e), e).start()

        @pl.when(s == 6)
        def _():
            small_copy(2, ag).wait_recv()
            for k in range(16):
                total[4 * k : 4 * k + 4] = ag[k]
            mat, guess = damp(total[...], tokens)
            inverse = newton(mat, guess, 0, NEWTON)
            top, bottom = inverse[:64], inverse[64:]
            weights[0], weights[1] = split2(jnp.concatenate([top, pltpu.roll(top, 64, 1)], axis=0))
            weights[2], weights[3] = split2(jnp.concatenate([pltpu.roll(bottom, 64, 1), bottom], axis=0))

        pl.when(s == STOPS)(land)

        @pl.loop(jnp.where(s == 8, 8, 0), jnp.where(s <= 6, 0, 8 * (s - 6)))
        def _(j):
            query_batch(j)

        pl.when(s == STOPS)(pass_on)

    for e in range(4):
        grad_copy(0, e).wait_recv()

    @pl.loop(0, 2)
    def _(i):
        at = pl.multiple_of(zhi * 512, 512)
        to = pl.multiple_of(i * 256, 256)
        tile = lax.dot_general(
            grads[pl.ds(at, 512), :], pre[pl.ds(to, 256), :], (((1,), (1,)), ((), ())), preferred_element_type=F32
        )
        out_ref[pl.ds(at, 512), pl.ds(to, 256)] = tile * 0.125

    @pl.loop(0, 4)
    def _(i):
        e = jnp.where(i == 2, 3, jnp.where(i == 3, 2, i))

        @pl.when(i == 1)
        def _():
            fy(1, 1, 2).wait_recv()

        @pl.when(i == 2)
        def _():
            fy(3, 0, 3).wait_recv()

        @pl.when(i == 3)
        def _():
            for k in range(CHUNKS):
                fyc(2, 0, k, 2).wait_recv()
                fyc(2, 1, k, 3).wait_recv()

        row = far_rows + 128 * i + 64 * c
        form(far(e), row)
        grad_copy(row, 4 + i).start()

    @pl.loop(0, 2)
    def _(i):
        grad_copy(0, 4 + 2 * i).wait_recv()
        grad_copy(0, 5 + 2 * i).wait_recv()
        at = pl.multiple_of(far_rows + 256 * i, 256)
        tile = lax.dot_general(
            grads[pl.ds(at, 256), :], pre[...], (((1,), (1,)), ((), ())), preferred_element_type=F32
        )
        for k in range(2):
            to = far_rows + 128 * jnp.where(i == 0, far_y[k], far_y[2 + k])
            out_ref[pl.ds(pl.multiple_of(to, 128), 128), :] = tile[128 * k : 128 * k + 128] * 0.125

    for d in (1, 2, 3):
        units = qbuf.at[pl.ds(0, ZLO)]
        copy(units, units, x_s.at[d - 1], x_r.at[d - 1]).wait_send()
        copy(block(0), block(0), y_s.at[d - 1], y_r.at[d - 1]).wait_send()
    for i in (2, 3):
        fy(0, 0, i).wait_send()
    for i in range(4):
        for k in range(CHUNKS):
            fyc(0, 0, k, i).wait_send()
    for stage, buf in ((0, rs), (1, zs), (2, ag)):
        small_copy(stage, buf).wait_send()

    @pl.loop(0, 8)
    def _(s):
        grad_copy(0, s).wait_send()

        @pl.when(s < STOPS)
        def _():
            for d in range(2):
                for k in range(CHUNKS):
                    i = ring_index(d, s) + k
                    slot = tbuf.at[0, pl.ds(0, rows)]
                    copy(slot, slot, ring_s.at[i], ring_r.at[i]).wait_send()

        @pl.when((zlo >= s) & (zlo < ZLO - 1))
        def _():
            copy(qbuf.at[0], qbuf.at[0], ku_s.at[s], ku_r.at[s]).wait_send()

        @pl.when((zlo + s <= ZLO - 1) & (zlo > 0))
        def _():
            copy(qbuf.at[0], qbuf.at[0], kd_s.at[s], kd_r.at[s]).wait_send()


def body(train_factors, query_factors):
    tokens = train_factors.shape[0] * train_factors.shape[1] * 512
    train = pltpu.with_memory_space_constraint(train_factors.reshape(-1, 128), pltpu.HBM)
    query = pltpu.with_memory_space_constraint(query_factors.reshape(-1, 128), pltpu.HBM)
    hbm = pl.BlockSpec(memory_space=pltpu.HBM)
    dma = pltpu.SemaphoreType.DMA
    return pl.pallas_call(
        functools.partial(kernel, tokens),
        out_shape=jax.ShapeDtypeStruct((1024, 512), F32),
        in_specs=[hbm, hbm],
        out_specs=pl.BlockSpec(memory_space=pltpu.VMEM),
        scratch_shapes=[
            pltpu.VMEM((1024, 128), BF16),
            pltpu.VMEM((256, 128), BF16),
            pltpu.VMEM((STAGE + 14, HALF, 128), BF16),
            pltpu.VMEM((32, UNIT, 128), BF16),
            pltpu.VMEM((1024, 4096), BF16),
            pltpu.VMEM((512, 4096), BF16),
            pltpu.VMEM((64, 128), F32),
            pltpu.VMEM((64, 128), F32),
            pltpu.VMEM((16, 4, 128), F32),
            pltpu.VMEM((16, 4, 128), F32),
            pltpu.VMEM((16, 4, 128), F32),
            pltpu.VMEM((16, 4, 128), F32),
            pltpu.VMEM((64, 128), F32),
            pltpu.VMEM((4, 128, 128), BF16),
            dma((2,)), dma, dma, dma((3,)), dma((3,)), dma((16 * CHUNKS,)), dma((16 * CHUNKS,)),
            dma((9,)), dma((9,)), dma((9,)), dma((9,)), dma((3,)), dma((48,)), dma((3,)), dma((3,)), dma((14,)), dma((14,)),
            dma((8,)), dma((8,)),
        ],
        compiler_params=pltpu.CompilerParams(
            collective_id=0, has_side_effects=True, vmem_limit_bytes=48 * 2**20
        ),
        name="influence",
    )(train, query)


def solution(mesh):
    return jax.shard_map(
        body,
        mesh=mesh,
        in_specs=(P(("train", "query"), None, None), P(("query", "train"), None, None)),
        out_specs=P("train", "query"),
        check_vma=False,
    )
```

```python
import functools

import jax
import jax.numpy as jnp
from jax import lax
from jax.experimental import pallas as pl
from jax.experimental.pallas import tpu as pltpu
from jax.sharding import PartitionSpec as P

MESH = pl.DeviceIdType.MESH
F32 = jnp.float32
BF16 = jnp.bfloat16

NX, NY, NZ, ZLO = 4, 4, 16, 8
UNIT = 256
HALF = 512
STAGE = 32
CHUNKS = 2
STOPS = 8
NEWTON = 8
LOW, HIGH = 0.1, 64.1


def coordinates():
    t = lax.axis_index("train")
    q = lax.axis_index("query")
    return t // ZLO, (q // 2) % NY, (q // (2 * NY)) * ZLO + t % ZLO, q % 2


def device(x, y, z, c):
    return (x * ZLO + z % ZLO, (z // ZLO) * (2 * NY) + y * 2 + c)


def iota(shape, dim):
    return lax.broadcasted_iota(jnp.int32, shape, dim)


def split2(v):
    hi = v.astype(BF16)
    return hi, (v - hi.astype(F32)).astype(BF16)


def mm(a, b):
    return jnp.dot(a, b, preferred_element_type=F32)


def mm3(a, b):
    ah, al = split2(a)
    bh, bl = split2(b)
    return mm(ah, bh) + (mm(ah, bl) + mm(al, bh))


def mmh(a, b):
    return jnp.dot(a, b, preferred_element_type=F32, precision=lax.Precision.HIGHEST)


def eye128():
    return jnp.where(iota((128, 128), 0) == iota((128, 128), 1), 1.0, 0.0)


def damp(total, tokens):
    row, lane = iota((64, 128), 0), iota((64, 128), 1)
    cov = total * (1.0 / tokens)
    first = lane < 64
    tr_in = jnp.sum(jnp.where(lane == row, cov, 0.0)) * (1.0 / 64)
    tr_out = jnp.sum(jnp.where(lane == row + 64, cov, 0.0)) * (1.0 / 64)
    top = jnp.where(first, cov + jnp.where(lane == row, 0.1 * tr_in, 0.0), 0.0)
    bottom = jnp.where(first, 0.0, cov + jnp.where(lane == row + 64, 0.1 * tr_out, 0.0))
    r, lanes = iota((128, 128), 0), iota((128, 128), 1)
    mean = jnp.where(r < 64, tr_in, tr_out)
    guess = jnp.where(r == lanes, (2.0 / (LOW + HIGH)) / mean, 0.0)
    return jnp.concatenate([top, bottom], axis=0), guess


def newton(damped, inv, lo, hi):
    bound = 2.0 * LOW / (LOW + HIGH)
    for step in range(hi):
        mapped = bound * (2.0 - bound)
        plain = step >= NEWTON - 2
        if step >= lo:
            mul = mmh if plain else mm3
            inv = mul(inv, 2.0 * eye128() - mul(damped, inv))
            if not plain:
                inv = inv * (2.0 / (1.0 + mapped))
        bound = 2.0 * mapped / (1.0 + mapped)
    return inv


def expand(first_t, mask):
    rows = []
    for i in range(32):
        a = jnp.broadcast_to(first_t[i : i + 1], (8, 128)) * mask
        b = jnp.broadcast_to(first_t[32 + i : 33 + i], (8, 128)) * mask
        rows.append(jnp.concatenate([a, b], axis=1))
    return jnp.concatenate(rows, axis=0)


def spread(second, rolled, group):
    left = iota((128, 128), 1) < 64
    zero = jnp.zeros_like(second)
    if group == 0:
        return jnp.concatenate([jnp.where(left, second, zero), jnp.where(left, zero, rolled)], axis=0)
    return jnp.concatenate([jnp.where(left, rolled, zero), jnp.where(left, zero, second)], axis=0)


def store_rows(out_ref, row, pair):
    a, b = pair
    for i in range(32):
        tile = jnp.concatenate([a[8 * i : 8 * i + 8], b[8 * i : 8 * i + 8]], axis=0)
        out_ref[pl.ds(row, 16), 128 * i : 128 * i + 128] = tile.astype(BF16)


def kernel(
    tokens, train_hbm, query_hbm, out_ref, train_ref, query_ref, tbuf, qbuf, grads, pre, part, sibpart, half, rs, zs,
    ag, total, weights, in_sem, sib_s, sib_r, small_s, small_r, ring_s, ring_r, ku_s, ku_r, kd_s, kd_r, x_s, x_r,
    y_s, y_r, fy_s, fy_r, g_s, g_r,
):
    x, y, z, c = coordinates()
    me_t = lax.axis_index("train")
    me_q = lax.axis_index("query")
    plane = x * NY + y
    sibling = device(x, y, z, 1 - c)
    zlo = lax.rem(z, ZLO)
    zhi = z // ZLO
    plane_peers = [
        (lax.rem(x + dx, NX), lax.rem(y + dy, NY)) for dx in range(NX) for dy in range(NY) if dx or dy
    ]
    plane_to = [device(px, py, z, c) for px, py in plane_peers]
    z_to = [device(x, y, lax.rem(z + dz, NZ), c) for dz in range(1, NZ)]
    x_to = [device(lax.rem(x + d, NX), y, z, c) for d in range(NX)]
    y_to = [device(x, lax.rem(y + d, NY), z, c) for d in range(NY)]

    inputs = [
        pltpu.make_async_copy(train_hbm, train_ref, in_sem.at[0]),
        pltpu.make_async_copy(query_hbm, query_ref, in_sem.at[1]),
    ]
    for cp in inputs:
        cp.start()
    barrier = pltpu.get_barrier_semaphore()
    for to in [*z_to, *plane_to, sibling]:
        pl.semaphore_signal(barrier, inc=1, device_id=to, device_id_type=MESH)
    for cp in inputs:
        cp.wait()

    left = iota((128, 128), 1) < 64

    def arrange(src, at, dst, block, to):
        a = src[pl.ds(at, 128), :]
        b = src[pl.ds(at + 128, 128), :]
        a32, b32 = a.astype(F32), b.astype(F32)
        at32, bt32 = a32.T, b32.T
        dst[block, pl.ds(to, 64), :] = at32[:64].astype(BF16)
        dst[block, pl.ds(to + 64, 64), :] = bt32[:64].astype(BF16)
        dst[block, pl.ds(to + 128, 128), :] = jnp.where(left, pltpu.roll(a32, 64, 1), b32).astype(BF16)
        return a, b, at32.astype(BF16), bt32.astype(BF16)

    cov = jnp.zeros((128, 128), F32)
    for u in range(4):
        a, b, at, bt = arrange(train_ref, u * UNIT, tbuf, 2 * me_q + u // 2, (u % 2) * UNIT)
        cov = cov + mm(at, a) + mm(bt, b)
    arrange(query_ref, 0, qbuf, me_t, 0)
    part[...] = jnp.where(iota((64, 128), 1) < 64, cov[:64], cov[64:])

    pl.semaphore_wait(barrier, 31)

    def copy(src, dst, ssem, rsem, to=sibling):
        return pltpu.make_async_remote_copy(
            src_ref=src, dst_ref=dst, send_sem=ssem, recv_sem=rsem, device_id=to, device_id_type=MESH
        )

    rows = HALF // CHUNKS

    def ring_index(d, step):
        return (step * 2 + d) * CHUNKS

    def ring_slot(d, step, k):
        landed = 2 * lax.rem(me_q + 8, 16) + d
        return tbuf.at[jnp.where(step < STOPS - 1, STAGE + d * 7 + step, landed), pl.ds(rows * k, rows)]

    def ring_send(d, step, k, src):
        zr = lax.rem(z + (1 if d == 0 else NZ - 1), NZ)
        landed = 2 * ((1 - zr // ZLO) * 8 + 2 * y + c) + d
        dst = tbuf.at[jnp.where(step < STOPS - 1, STAGE + d * 7 + step, landed), pl.ds(rows * k, rows)]
        i = ring_index(d, step) + k
        copy(src, dst, ring_s, ring_r.at[i], device(x, y, zr, c)).start()

    def ring_recv(d, step, k):
        i = ring_index(d, step) + k
        slot = ring_slot(d, step, k)
        copy(slot, slot, ring_s, ring_r.at[i]).wait_recv()
        return slot

    def chain_units(s):
        return me_t - jnp.minimum(s, zlo), me_t + jnp.minimum(s, ZLO - 1 - zlo)

    def chain_send(s):
        up, down = chain_units(s)

        @pl.when((zlo >= s) & (zlo < ZLO - 1))
        def _():
            to = device(x, y, jnp.minimum(z + 1, NZ - 1), c)
            copy(qbuf.at[up], qbuf.at[up], ku_s.at[s], ku_r.at[s], to).start()

        @pl.when((zlo + s <= ZLO - 1) & (zlo > 0))
        def _():
            to = device(x, y, jnp.maximum(z - 1, 0), c)
            copy(qbuf.at[down], qbuf.at[down], kd_s.at[s], kd_r.at[s], to).start()

    def chain_recv(s):
        up, down = chain_units(s)

        @pl.when(zlo >= s)
        def _():
            copy(qbuf.at[up], qbuf.at[up], ku_s.at[s - 1], ku_r.at[s - 1]).wait_recv()

        @pl.when(zlo + s <= ZLO - 1)
        def _():
            copy(qbuf.at[down], qbuf.at[down], kd_s.at[s - 1], kd_r.at[s - 1]).wait_recv()

    def x_send(unit, j):
        for d in (1, 2, 3):
            copy(qbuf.at[unit], qbuf.at[unit], x_s.at[d - 1], x_r.at[16 * (d - 1) + j], x_to[d]).start()

    def block(b):
        return tbuf.at[pl.ds(2 * b, 2)]

    def near(e):
        other = e // 4
        return me_q - lax.rem(me_q, 8) + 2 * lax.rem(y + NY - lax.rem(e, 4), NY) + (c + other - 2 * c * other)

    def far(e):
        return lax.rem(near(e) + 8, 16)

    copy(part, sibpart, sib_s, sib_r).start()
    for k in range(CHUNKS):
        for d in range(2):
            ring_send(d, 0, k, tbuf.at[2 * me_q + d, pl.ds(rows * k, rows)])
    chain_send(0)
    for d in (1, 2, 3):
        copy(block(me_q), block(me_q), y_s.at[d - 1], y_r.at[d - 1], y_to[d]).start()
    x_send(me_t, 0)

    copy(part, sibpart, sib_s, sib_r).wait()
    mine = part[...] + sibpart[...]
    for k in range(16):
        half[k] = mine[4 * k : 4 * k + 4]

    def small(stage, sources, dst, slot, peers):
        for src, to in zip(sources, peers, strict=True):
            copy(src, dst.at[slot], small_s.at[stage], small_r.at[stage], to).start()

    def small_copy(stage, buf):
        return copy(buf.at[pl.ds(0, 15)], buf.at[pl.ds(0, 15)], small_s.at[stage], small_r.at[stage])

    def sum16(buf):
        piece = buf[0]
        for k in range(1, 16):
            piece = piece + buf[k]
        return piece

    small(0, [half.at[px * NY + py] for px, py in plane_peers], rs, plane, plane_to)
    rs[plane] = half[plane]

    mask = jnp.where(iota((8, 128), 1) // 16 == iota((8, 128), 0), 1.0 / 16, 0.0)

    def form_half(hb, row):
        for u in range(2):
            second = tbuf[hb, u * UNIT + 128 : u * UNIT + 256, :]
            rolled = pltpu.roll(second.astype(F32), 64, 1).astype(BF16)
            outs = []
            for g in range(2):
                first = tbuf[hb, u * UNIT + 64 * g : u * UNIT + 64 * g + 64, :]
                lhs = expand(first.astype(F32), mask).astype(BF16)
                outs.append(mm(lhs, spread(second, rolled, g)))
            store_rows(grads, pl.multiple_of(row + u * 16, 16), outs)

    def form(b, row):
        form_half(2 * b, row)
        form_half(2 * b + 1, row + 32)

    def grad_copy(row, i):
        rows_of = grads.at[pl.ds(pl.multiple_of(row, 64), 64)]
        return copy(rows_of, rows_of, g_s.at[i], g_r.at[i])

    far_rows = (1 - zhi) * 512
    far_y = [y, lax.rem(y + 3, NY), lax.rem(y + 1, NY), lax.rem(y + 2, NY)]

    def query_units(units):
        firsts, seconds = [], []
        for b in units:
            first = qbuf[b, 0:128, :]
            second = qbuf[b, 128:256, :]
            firsts.append(mm(weights[0], first) + mm(weights[1], first))
            seconds.append(mm(second, weights[2]) + mm(second, weights[3]))
        for b, first_p, second_p in zip(units, firsts, seconds, strict=True):
            rolled = pltpu.roll(second_p, 64, 1)
            outs = []
            for g in range(2):
                lhs_h, lhs_l = split2(expand(first_p[64 * g : 64 * g + 64], mask))
                rhs_h, rhs_l = split2(spread(second_p, rolled, g))
                both = mm(lhs_h, jnp.concatenate([rhs_h, rhs_l], axis=1))
                outs.append(both[:, :128] + both[:, 128:] + mm(lhs_l, rhs_h))
            store_rows(pre, pl.multiple_of(b * 16, 16), outs)

    def query_batch(j):
        far_z = j // 2
        above = j % 2 == 1
        shift = jnp.where(above, far_z, -far_z)

        @pl.when((above & (far_z > 0) & (zlo + far_z <= ZLO - 1)) | (jnp.logical_not(above) & (zlo >= far_z)))
        def _():
            units = [lax.rem(x + NX - d, NX) * ZLO + zlo + shift for d in range(NX)]
            for d in (1, 2, 3):
                b = qbuf.at[units[d]]
                copy(b, b, x_s.at[d - 1], x_r.at[16 * (d - 1) + j]).wait_recv()
            query_units(units)

    def far_half(e, d):
        return tbuf.at[2 * far(e) + d]

    def fy(e, d, i, to=0):
        return copy(far_half(e, d), far_half(e, d), fy_s.at[i], fy_r.at[i], y_to[to])

    def fyc(e, d, k, i, to=0):
        part_of = tbuf.at[2 * far(e) + d, pl.ds(rows * k, rows)]
        j = 6 + 2 * i + k
        return copy(part_of, part_of, fy_s.at[j], fy_r.at[j], y_to[to])

    def land():
        for k in range(CHUNKS):
            for d in range(2):
                ring_recv(d, STOPS - 1, k)
                fyc(0, d, k, d, 1 if d == 0 else 3).start()
        fy(0, 1, 2, 1).start()
        fy(0, 0, 3, 3).start()

    def pass_on():
        for k in range(CHUNKS):
            fyc(1, 0, k, 0).wait_recv()
            fyc(1, 0, k, 2, 1).start()
            fyc(3, 1, k, 1).wait_recv()
            fyc(3, 1, k, 3, 3).start()

    @pl.loop(1, 9)
    def _(s):
        @pl.when(s < STOPS)
        def _():
            for k in range(CHUNKS):
                for d in range(2):
                    ring_send(d, s, k, ring_recv(d, s - 1, k))

        chain_recv(s)
        chain_send(s)

        up, down = chain_units(s)
        pl.when(zlo >= s)(lambda: x_send(up, 2 * s))
        pl.when(zlo + s <= ZLO - 1)(lambda: x_send(down, 2 * s + 1))

        @pl.when(s == 2)
        def _():
            small_copy(0, rs).wait_recv()
            zs[z] = sum16(rs)
            small(1, [zs.at[z]] * 15, zs, z, z_to)

        @pl.when(s == 5)
        def _():
            small_copy(1, zs).wait_recv()
            ag[plane] = sum16(zs)
            small(2, [ag.at[plane]] * 15, ag, plane, plane_to)

        e = s - 1

        @pl.when((e >= 1) & (e <= 3))
        def _():
            copy(block(near(e)), block(near(e)), y_s.at[e - 1], y_r.at[e - 1]).wait_recv()

        @pl.when(e <= 3)
        def _():
            form(near(e), 64 * near(e))
            grad_copy(64 * near(e), e).start()

        @pl.when(s == 6)
        def _():
            small_copy(2, ag).wait_recv()
            for k in range(16):
                total[4 * k : 4 * k + 4] = ag[k]
            mat, guess = damp(total[...], tokens)
            inverse = newton(mat, guess, 0, NEWTON)
            top, bottom = inverse[:64], inverse[64:]
            weights[0], weights[1] = split2(jnp.concatenate([top, pltpu.roll(top, 64, 1)], axis=0))
            weights[2], weights[3] = split2(jnp.concatenate([pltpu.roll(bottom, 64, 1), bottom], axis=0))

        pl.when(s == STOPS)(land)

        @pl.loop(jnp.where(s == 8, 8, 0), jnp.where(s <= 6, 0, 8 * (s - 6)))
        def _(j):
            query_batch(j)

        pl.when(s == STOPS)(pass_on)

    for e in range(4):
        grad_copy(0, e).wait_recv()

    @pl.loop(0, 2)
    def _(i):
        at = pl.multiple_of(zhi * 512, 512)
        to = pl.multiple_of(i * 256, 256)
        tile = lax.dot_general(
            grads[pl.ds(at, 512), :], pre[pl.ds(to, 256), :], (((1,), (1,)), ((), ())), preferred_element_type=F32
        )
        out_ref[pl.ds(at, 512), pl.ds(to, 256)] = tile * 0.125

    ring_all = tbuf.at[pl.ds(0, 2 * STOPS)]
    copy(ring_all, ring_all, ring_s, ring_r.at[0]).wait_send()
    for d in (1, 2, 3):
        units = qbuf.at[pl.ds(0, ZLO)]
        copy(units, units, x_s.at[d - 1], x_r.at[d - 1]).wait_send()
        copy(block(0), block(0), y_s.at[d - 1], y_r.at[d - 1]).wait_send()
    for stage, buf in ((0, rs), (1, zs), (2, ag)):
        small_copy(stage, buf).wait_send()

    @pl.loop(0, 8)
    def _(s):
        @pl.when((zlo >= s) & (zlo < ZLO - 1))
        def _():
            copy(qbuf.at[0], qbuf.at[0], ku_s.at[s], ku_r.at[s]).wait_send()

        @pl.when((zlo + s <= ZLO - 1) & (zlo > 0))
        def _():
            copy(qbuf.at[0], qbuf.at[0], kd_s.at[s], kd_r.at[s]).wait_send()

    @pl.loop(0, 4)
    def _(i):
        e = jnp.where(i == 2, 3, jnp.where(i == 3, 2, i))

        @pl.when(i == 1)
        def _():
            fy(1, 1, 2).wait_recv()

        @pl.when(i == 2)
        def _():
            fy(3, 0, 3).wait_recv()

        @pl.when(i == 3)
        def _():
            for k in range(CHUNKS):
                fyc(2, 0, k, 2).wait_recv()
                fyc(2, 1, k, 3).wait_recv()

        row = far_rows + 128 * i + 64 * c
        form(far(e), row)
        grad_copy(row, 4 + i).start()

    @pl.loop(0, 2)
    def _(i):
        grad_copy(0, 4 + 2 * i).wait_recv()
        grad_copy(0, 5 + 2 * i).wait_recv()
        at = pl.multiple_of(far_rows + 256 * i, 256)
        tile = lax.dot_general(
            grads[pl.ds(at, 256), :], pre[...], (((1,), (1,)), ((), ())), preferred_element_type=F32
        )
        for k in range(2):
            to = far_rows + 128 * jnp.where(i == 0, far_y[k], far_y[2 + k])
            out_ref[pl.ds(pl.multiple_of(to, 128), 128), :] = tile[128 * k : 128 * k + 128] * 0.125

    for i in (2, 3):
        fy(0, 0, i).wait_send()
    for i in range(4):
        for k in range(CHUNKS):
            fyc(0, 0, k, i).wait_send()
    for i in range(8):
        grad_copy(0, i).wait_send()


def body(train_factors, query_factors):
    tokens = train_factors.shape[0] * train_factors.shape[1] * 512
    train = pltpu.with_memory_space_constraint(train_factors.reshape(-1, 128), pltpu.HBM)
    query = pltpu.with_memory_space_constraint(query_factors.reshape(-1, 128), pltpu.HBM)
    hbm = pl.BlockSpec(memory_space=pltpu.HBM)
    dma = pltpu.SemaphoreType.DMA
    return pl.pallas_call(
        functools.partial(kernel, tokens),
        out_shape=jax.ShapeDtypeStruct((1024, 512), F32),
        in_specs=[hbm, hbm],
        out_specs=pl.BlockSpec(memory_space=pltpu.VMEM),
        scratch_shapes=[
            pltpu.VMEM((1024, 128), BF16),
            pltpu.VMEM((256, 128), BF16),
            pltpu.VMEM((STAGE + 14, HALF, 128), BF16),
            pltpu.VMEM((32, UNIT, 128), BF16),
            pltpu.VMEM((1024, 4096), BF16),
            pltpu.VMEM((512, 4096), BF16),
            pltpu.VMEM((64, 128), F32),
            pltpu.VMEM((64, 128), F32),
            pltpu.VMEM((16, 4, 128), F32),
            pltpu.VMEM((16, 4, 128), F32),
            pltpu.VMEM((16, 4, 128), F32),
            pltpu.VMEM((16, 4, 128), F32),
            pltpu.VMEM((64, 128), F32),
            pltpu.VMEM((4, 128, 128), BF16),
            dma((2,)), dma, dma, dma((3,)), dma((3,)), dma, dma((16 * CHUNKS,)),
            dma((9,)), dma((9,)), dma((9,)), dma((9,)), dma((3,)), dma((48,)), dma((3,)), dma((3,)), dma((14,)), dma((14,)),
            dma((8,)), dma((8,)),
        ],
        compiler_params=pltpu.CompilerParams(
            collective_id=0, has_side_effects=True, vmem_limit_bytes=48 * 2**20
        ),
        name="influence",
    )(train, query)


def solution(mesh):
    return jax.shard_map(
        body,
        mesh=mesh,
        in_specs=(P(("train", "query"), None, None), P(("query", "train"), None, None)),
        out_specs=P("train", "query"),
        check_vma=False,
    )
```

```python
import functools

import jax
import jax.numpy as jnp
from jax import lax
from jax.experimental import pallas as pl
from jax.experimental.pallas import tpu as pltpu
from jax.sharding import PartitionSpec as P

MESH = pl.DeviceIdType.MESH
F32 = jnp.float32
BF16 = jnp.bfloat16

NX, NY, NZ, ZLO = 4, 4, 16, 8
UNIT = 256
HALF = 512
STAGE = 32
CHUNKS = 2
STOPS = 8
NEWTON = 8
LOW, HIGH = 0.1, 64.1


def coordinates():
    t = lax.axis_index("train")
    q = lax.axis_index("query")
    return t // ZLO, (q // 2) % NY, (q // (2 * NY)) * ZLO + t % ZLO, q % 2


def device(x, y, z, c):
    return (x * ZLO + z % ZLO, (z // ZLO) * (2 * NY) + y * 2 + c)


def iota(shape, dim):
    return lax.broadcasted_iota(jnp.int32, shape, dim)


def split2(v):
    hi = v.astype(BF16)
    return hi, (v - hi.astype(F32)).astype(BF16)


def mm(a, b):
    return jnp.dot(a, b, preferred_element_type=F32)


def mm3(a, b):
    ah, al = split2(a)
    bh, bl = split2(b)
    return mm(ah, bh) + (mm(ah, bl) + mm(al, bh))


def mmh(a, b):
    return jnp.dot(a, b, preferred_element_type=F32, precision=lax.Precision.HIGHEST)


def eye128():
    return jnp.where(iota((128, 128), 0) == iota((128, 128), 1), 1.0, 0.0)


def damp(total, tokens):
    row, lane = iota((64, 128), 0), iota((64, 128), 1)
    cov = total * (1.0 / tokens)
    first = lane < 64
    tr_in = jnp.sum(jnp.where(lane == row, cov, 0.0)) * (1.0 / 64)
    tr_out = jnp.sum(jnp.where(lane == row + 64, cov, 0.0)) * (1.0 / 64)
    top = jnp.where(first, cov + jnp.where(lane == row, 0.1 * tr_in, 0.0), 0.0)
    bottom = jnp.where(first, 0.0, cov + jnp.where(lane == row + 64, 0.1 * tr_out, 0.0))
    r, lanes = iota((128, 128), 0), iota((128, 128), 1)
    mean = jnp.where(r < 64, tr_in, tr_out)
    guess = jnp.where(r == lanes, (2.0 / (LOW + HIGH)) / mean, 0.0)
    return jnp.concatenate([top, bottom], axis=0), guess


def newton(damped, inv, lo, hi):
    bound = 2.0 * LOW / (LOW + HIGH)
    for step in range(hi):
        mapped = bound * (2.0 - bound)
        plain = step >= NEWTON - 2
        if step >= lo:
            mul = mmh if plain else mm3
            inv = mul(inv, 2.0 * eye128() - mul(damped, inv))
            if not plain:
                inv = inv * (2.0 / (1.0 + mapped))
        bound = 2.0 * mapped / (1.0 + mapped)
    return inv


def expand(first_t, mask):
    rows = []
    for i in range(32):
        a = jnp.broadcast_to(first_t[i : i + 1], (8, 128)) * mask
        b = jnp.broadcast_to(first_t[32 + i : 33 + i], (8, 128)) * mask
        rows.append(jnp.concatenate([a, b], axis=1))
    return jnp.concatenate(rows, axis=0)


def spread(second, rolled, group):
    left = iota((128, 128), 1) < 64
    zero = jnp.zeros_like(second)
    if group == 0:
        return jnp.concatenate([jnp.where(left, second, zero), jnp.where(left, zero, rolled)], axis=0)
    return jnp.concatenate([jnp.where(left, rolled, zero), jnp.where(left, zero, second)], axis=0)


def store_rows(out_ref, row, pair):
    a, b = pair
    for i in range(32):
        tile = jnp.concatenate([a[8 * i : 8 * i + 8], b[8 * i : 8 * i + 8]], axis=0)
        out_ref[pl.ds(row, 16), 128 * i : 128 * i + 128] = tile.astype(BF16)


def kernel(
    tokens, train_hbm, query_hbm, out_ref, train_ref, query_ref, tbuf, qbuf, grads, pre, part, sibpart, half, rs, zs,
    ag, total, weights, in_sem, sib_s, sib_r, small_s, small_r, ring_s, ring_r, ku_s, ku_r, kd_s, kd_r, x_s, x_r,
    y_s, y_r, fy_s, fy_r, g_s, g_r,
):
    x, y, z, c = coordinates()
    me_t = lax.axis_index("train")
    me_q = lax.axis_index("query")
    plane = x * NY + y
    sibling = device(x, y, z, 1 - c)
    zlo = lax.rem(z, ZLO)
    zhi = z // ZLO
    plane_peers = [
        (lax.rem(x + dx, NX), lax.rem(y + dy, NY)) for dx in range(NX) for dy in range(NY) if dx or dy
    ]
    plane_to = [device(px, py, z, c) for px, py in plane_peers]
    z_to = [device(x, y, lax.rem(z + dz, NZ), c) for dz in range(1, NZ)]
    x_to = [device(lax.rem(x + d, NX), y, z, c) for d in range(NX)]
    y_to = [device(x, lax.rem(y + d, NY), z, c) for d in range(NY)]

    inputs = [
        pltpu.make_async_copy(train_hbm, train_ref, in_sem.at[0]),
        pltpu.make_async_copy(query_hbm, query_ref, in_sem.at[1]),
    ]
    for cp in inputs:
        cp.start()
    barrier = pltpu.get_barrier_semaphore()
    for to in [*z_to, *plane_to, sibling]:
        pl.semaphore_signal(barrier, inc=1, device_id=to, device_id_type=MESH)
    for cp in inputs:
        cp.wait()

    left = iota((128, 128), 1) < 64

    def arrange(src, at, dst, block, to):
        a = src[pl.ds(at, 128), :]
        b = src[pl.ds(at + 128, 128), :]
        a32, b32 = a.astype(F32), b.astype(F32)
        at32, bt32 = a32.T, b32.T
        dst[block, pl.ds(to, 64), :] = at32[:64].astype(BF16)
        dst[block, pl.ds(to + 64, 64), :] = bt32[:64].astype(BF16)
        dst[block, pl.ds(to + 128, 128), :] = jnp.where(left, pltpu.roll(a32, 64, 1), b32).astype(BF16)
        return a, b, at32.astype(BF16), bt32.astype(BF16)

    cov = jnp.zeros((128, 128), F32)
    for u in range(4):
        a, b, at, bt = arrange(train_ref, u * UNIT, tbuf, 2 * me_q + u // 2, (u % 2) * UNIT)
        cov = cov + mm(at, a) + mm(bt, b)
    arrange(query_ref, 0, qbuf, me_t, 0)
    part[...] = jnp.where(iota((64, 128), 1) < 64, cov[:64], cov[64:])

    pl.semaphore_wait(barrier, 31)

    def copy(src, dst, ssem, rsem, to=sibling):
        return pltpu.make_async_remote_copy(
            src_ref=src, dst_ref=dst, send_sem=ssem, recv_sem=rsem, device_id=to, device_id_type=MESH
        )

    rows = HALF // CHUNKS

    def ring_index(d, step):
        return (step * 2 + d) * CHUNKS

    def ring_slot(d, step, k):
        landed = 2 * lax.rem(me_q + 8, 16) + d
        return tbuf.at[jnp.where(step < STOPS - 1, STAGE + d * 7 + step, landed), pl.ds(rows * k, rows)]

    def ring_send(d, step, k, src):
        zr = lax.rem(z + (1 if d == 0 else NZ - 1), NZ)
        landed = 2 * ((1 - zr // ZLO) * 8 + 2 * y + c) + d
        dst = tbuf.at[jnp.where(step < STOPS - 1, STAGE + d * 7 + step, landed), pl.ds(rows * k, rows)]
        i = ring_index(d, step) + k
        copy(src, dst, ring_s, ring_r.at[i], device(x, y, zr, c)).start()

    def ring_recv(d, step, k):
        i = ring_index(d, step) + k
        slot = ring_slot(d, step, k)
        copy(slot, slot, ring_s, ring_r.at[i]).wait_recv()
        return slot

    def chain_units(s):
        return me_t - jnp.minimum(s, zlo), me_t + jnp.minimum(s, ZLO - 1 - zlo)

    def chain_send(s):
        up, down = chain_units(s)

        @pl.when((zlo >= s) & (zlo < ZLO - 1))
        def _():
            to = device(x, y, jnp.minimum(z + 1, NZ - 1), c)
            copy(qbuf.at[up], qbuf.at[up], ku_s.at[s], ku_r.at[s], to).start()

        @pl.when((zlo + s <= ZLO - 1) & (zlo > 0))
        def _():
            to = device(x, y, jnp.maximum(z - 1, 0), c)
            copy(qbuf.at[down], qbuf.at[down], kd_s.at[s], kd_r.at[s], to).start()

    def chain_recv(s):
        up, down = chain_units(s)

        @pl.when(zlo >= s)
        def _():
            copy(qbuf.at[up], qbuf.at[up], ku_s.at[s - 1], ku_r.at[s - 1]).wait_recv()

        @pl.when(zlo + s <= ZLO - 1)
        def _():
            copy(qbuf.at[down], qbuf.at[down], kd_s.at[s - 1], kd_r.at[s - 1]).wait_recv()

    def x_send(unit, j):
        for d in (1, 2, 3):
            copy(qbuf.at[unit], qbuf.at[unit], x_s.at[d - 1], x_r.at[16 * (d - 1) + j], x_to[d]).start()

    def block(b):
        return tbuf.at[pl.ds(2 * b, 2)]

    def near(e):
        other = e // 4
        return me_q - lax.rem(me_q, 8) + 2 * lax.rem(y + NY - lax.rem(e, 4), NY) + (c + other - 2 * c * other)

    def far(e):
        return lax.rem(near(e) + 8, 16)

    copy(part, sibpart, sib_s, sib_r).start()
    for k in range(CHUNKS):
        for d in range(2):
            ring_send(d, 0, k, tbuf.at[2 * me_q + d, pl.ds(rows * k, rows)])
    chain_send(0)

    copy(part, sibpart, sib_s, sib_r).wait()
    mine = part[...] + sibpart[...]
    for k in range(16):
        half[k] = mine[4 * k : 4 * k + 4]

    def small(stage, sources, dst, slot, peers):
        for src, to in zip(sources, peers, strict=True):
            copy(src, dst.at[slot], small_s.at[stage], small_r.at[stage], to).start()

    def small_copy(stage, buf):
        return copy(buf.at[pl.ds(0, 15)], buf.at[pl.ds(0, 15)], small_s.at[stage], small_r.at[stage])

    def sum16(buf):
        piece = buf[0]
        for k in range(1, 16):
            piece = piece + buf[k]
        return piece

    small(0, [half.at[px * NY + py] for px, py in plane_peers], rs, plane, plane_to)
    rs[plane] = half[plane]
    for d in (1, 2, 3):
        copy(block(me_q), block(me_q), y_s.at[d - 1], y_r.at[d - 1], y_to[d]).start()
    x_send(me_t, 0)

    mask = jnp.where(iota((8, 128), 1) // 16 == iota((8, 128), 0), 1.0 / 16, 0.0)

    def form_half(hb, row):
        for u in range(2):
            second = tbuf[hb, u * UNIT + 128 : u * UNIT + 256, :]
            rolled = pltpu.roll(second.astype(F32), 64, 1).astype(BF16)
            outs = []
            for g in range(2):
                first = tbuf[hb, u * UNIT + 64 * g : u * UNIT + 64 * g + 64, :]
                lhs = expand(first.astype(F32), mask).astype(BF16)
                outs.append(mm(lhs, spread(second, rolled, g)))
            store_rows(grads, pl.multiple_of(row + u * 16, 16), outs)

    def form(b, row):
        form_half(2 * b, row)
        form_half(2 * b + 1, row + 32)

    def grad_copy(row, i):
        rows_of = grads.at[pl.ds(pl.multiple_of(row, 64), 64)]
        return copy(rows_of, rows_of, g_s.at[i], g_r.at[i])

    far_rows = (1 - zhi) * 512
    far_y = [y, lax.rem(y + 3, NY), lax.rem(y + 1, NY), lax.rem(y + 2, NY)]

    def query_units(units):
        firsts, seconds = [], []
        for b in units:
            first = qbuf[b, 0:128, :]
            second = qbuf[b, 128:256, :]
            firsts.append(mm(weights[0], first) + mm(weights[1], first))
            seconds.append(mm(second, weights[2]) + mm(second, weights[3]))
        for b, first_p, second_p in zip(units, firsts, seconds, strict=True):
            rolled = pltpu.roll(second_p, 64, 1)
            outs = []
            for g in range(2):
                lhs_h, lhs_l = split2(expand(first_p[64 * g : 64 * g + 64], mask))
                rhs_h, rhs_l = split2(spread(second_p, rolled, g))
                both = mm(lhs_h, jnp.concatenate([rhs_h, rhs_l], axis=1))
                outs.append(both[:, :128] + both[:, 128:] + mm(lhs_l, rhs_h))
            store_rows(pre, pl.multiple_of(b * 16, 16), outs)

    def query_batch(j):
        far_z = j // 2
        above = j % 2 == 1
        shift = jnp.where(above, far_z, -far_z)

        @pl.when((above & (far_z > 0) & (zlo + far_z <= ZLO - 1)) | (jnp.logical_not(above) & (zlo >= far_z)))
        def _():
            units = [lax.rem(x + NX - d, NX) * ZLO + zlo + shift for d in range(NX)]
            for d in (1, 2, 3):
                b = qbuf.at[units[d]]
                copy(b, b, x_s.at[d - 1], x_r.at[16 * (d - 1) + j]).wait_recv()
            query_units(units)

    def far_half(e, d):
        return tbuf.at[2 * far(e) + d]

    def fy(e, d, i, to=0):
        return copy(far_half(e, d), far_half(e, d), fy_s.at[i], fy_r.at[i], y_to[to])

    def fyc(e, d, k, i, to=0):
        part_of = tbuf.at[2 * far(e) + d, pl.ds(rows * k, rows)]
        j = 6 + 2 * i + k
        return copy(part_of, part_of, fy_s.at[j], fy_r.at[j], y_to[to])

    def land():
        for k in range(CHUNKS):
            for d in range(2):
                ring_recv(d, STOPS - 1, k)
                fyc(0, d, k, d, 1 if d == 0 else 3).start()
        fy(0, 1, 2, 1).start()
        fy(0, 0, 3, 3).start()

    def pass_on():
        for k in range(CHUNKS):
            fyc(1, 0, k, 0).wait_recv()
            fyc(1, 0, k, 2, 1).start()
            fyc(3, 1, k, 1).wait_recv()
            fyc(3, 1, k, 3, 3).start()

    @pl.loop(1, 9)
    def _(s):
        @pl.when(s < STOPS)
        def _():
            for k in range(CHUNKS):
                for d in range(2):
                    ring_send(d, s, k, ring_recv(d, s - 1, k))

        chain_recv(s)
        chain_send(s)

        up, down = chain_units(s)
        pl.when(zlo >= s)(lambda: x_send(up, 2 * s))
        pl.when(zlo + s <= ZLO - 1)(lambda: x_send(down, 2 * s + 1))

        @pl.when(s == 2)
        def _():
            small_copy(0, rs).wait_recv()
            zs[z] = sum16(rs)
            small(1, [zs.at[z]] * 15, zs, z, z_to)

        @pl.when(s == 4)
        def _():
            small_copy(1, zs).wait_recv()
            ag[plane] = sum16(zs)
            small(2, [ag.at[plane]] * 15, ag, plane, plane_to)

        e = s - 1

        @pl.when((e >= 1) & (e <= 3))
        def _():
            copy(block(near(e)), block(near(e)), y_s.at[e - 1], y_r.at[e - 1]).wait_recv()

        @pl.when(e <= 3)
        def _():
            form(near(e), 64 * near(e))
            grad_copy(64 * near(e), e).start()

        @pl.when(s == 5)
        def _():
            small_copy(2, ag).wait_recv()
            for k in range(16):
                total[4 * k : 4 * k + 4] = ag[k]
            mat, guess = damp(total[...], tokens)
            inverse = newton(mat, guess, 0, NEWTON)
            top, bottom = inverse[:64], inverse[64:]
            weights[0], weights[1] = split2(jnp.concatenate([top, pltpu.roll(top, 64, 1)], axis=0))
            weights[2], weights[3] = split2(jnp.concatenate([pltpu.roll(bottom, 64, 1), bottom], axis=0))

        pl.when(s == STOPS)(land)

        wide = jnp.where((zlo <= 1) | (zlo >= ZLO - 2), 6, 4)

        @pl.loop(jnp.where(s <= 6, 0, wide * (s - 6)), jnp.where(s <= 5, 0, jnp.where(s == 8, 16, wide * (s - 5))))
        def _(j):
            query_batch(j)

        pl.when(s == STOPS)(pass_on)

    for e in range(4):
        grad_copy(0, e).wait_recv()

    @pl.loop(0, 2)
    def _(i):
        at = pl.multiple_of(zhi * 512, 512)
        to = pl.multiple_of(i * 256, 256)
        tile = lax.dot_general(
            grads[pl.ds(at, 512), :], pre[pl.ds(to, 256), :], (((1,), (1,)), ((), ())), preferred_element_type=F32
        )
        out_ref[pl.ds(at, 512), pl.ds(to, 256)] = tile * 0.125

    ring_all = tbuf.at[pl.ds(0, 2 * STOPS)]
    copy(ring_all, ring_all, ring_s, ring_r.at[0]).wait_send()
    for d in (1, 2, 3):
        units = qbuf.at[pl.ds(0, ZLO)]
        copy(units, units, x_s.at[d - 1], x_r.at[d - 1]).wait_send()
        copy(block(0), block(0), y_s.at[d - 1], y_r.at[d - 1]).wait_send()
    for stage, buf in ((0, rs), (1, zs), (2, ag)):
        small_copy(stage, buf).wait_send()

    @pl.loop(0, 8)
    def _(s):
        @pl.when((zlo >= s) & (zlo < ZLO - 1))
        def _():
            copy(qbuf.at[0], qbuf.at[0], ku_s.at[s], ku_r.at[s]).wait_send()

        @pl.when((zlo + s <= ZLO - 1) & (zlo > 0))
        def _():
            copy(qbuf.at[0], qbuf.at[0], kd_s.at[s], kd_r.at[s]).wait_send()

    @pl.loop(0, 4)
    def _(i):
        e = jnp.where(i == 2, 3, jnp.where(i == 3, 2, i))

        @pl.when(i == 1)
        def _():
            fy(1, 1, 2).wait_recv()

        @pl.when(i == 2)
        def _():
            fy(3, 0, 3).wait_recv()

        @pl.when(i == 3)
        def _():
            for k in range(CHUNKS):
                fyc(2, 0, k, 2).wait_recv()
                fyc(2, 1, k, 3).wait_recv()

        row = far_rows + 128 * i + 64 * c
        form(far(e), row)
        grad_copy(row, 4 + i).start()

    @pl.loop(0, 2)
    def _(i):
        grad_copy(0, 4 + 2 * i).wait_recv()
        grad_copy(0, 5 + 2 * i).wait_recv()
        at = pl.multiple_of(far_rows + 256 * i, 256)
        tile = lax.dot_general(
            grads[pl.ds(at, 256), :], pre[...], (((1,), (1,)), ((), ())), preferred_element_type=F32
        )
        for k in range(2):
            to = far_rows + 128 * jnp.where(i == 0, far_y[k], far_y[2 + k])
            out_ref[pl.ds(pl.multiple_of(to, 128), 128), :] = tile[128 * k : 128 * k + 128] * 0.125

    for i in (2, 3):
        fy(0, 0, i).wait_send()
    for i in range(4):
        for k in range(CHUNKS):
            fyc(0, 0, k, i).wait_send()
    for i in range(8):
        grad_copy(0, i).wait_send()


def body(train_factors, query_factors):
    tokens = train_factors.shape[0] * train_factors.shape[1] * 512
    train = pltpu.with_memory_space_constraint(train_factors.reshape(-1, 128), pltpu.HBM)
    query = pltpu.with_memory_space_constraint(query_factors.reshape(-1, 128), pltpu.HBM)
    hbm = pl.BlockSpec(memory_space=pltpu.HBM)
    dma = pltpu.SemaphoreType.DMA
    return pl.pallas_call(
        functools.partial(kernel, tokens),
        out_shape=jax.ShapeDtypeStruct((1024, 512), F32),
        in_specs=[hbm, hbm],
        out_specs=pl.BlockSpec(memory_space=pltpu.VMEM),
        scratch_shapes=[
            pltpu.VMEM((1024, 128), BF16),
            pltpu.VMEM((256, 128), BF16),
            pltpu.VMEM((STAGE + 14, HALF, 128), BF16),
            pltpu.VMEM((32, UNIT, 128), BF16),
            pltpu.VMEM((1024, 4096), BF16),
            pltpu.VMEM((512, 4096), BF16),
            pltpu.VMEM((64, 128), F32),
            pltpu.VMEM((64, 128), F32),
            pltpu.VMEM((16, 4, 128), F32),
            pltpu.VMEM((16, 4, 128), F32),
            pltpu.VMEM((16, 4, 128), F32),
            pltpu.VMEM((16, 4, 128), F32),
            pltpu.VMEM((64, 128), F32),
            pltpu.VMEM((4, 128, 128), BF16),
            dma((2,)), dma, dma, dma((3,)), dma((3,)), dma, dma((16 * CHUNKS,)),
            dma((9,)), dma((9,)), dma((9,)), dma((9,)), dma((3,)), dma((48,)), dma((3,)), dma((3,)), dma((14,)), dma((14,)),
            dma((8,)), dma((8,)),
        ],
        compiler_params=pltpu.CompilerParams(
            collective_id=0, has_side_effects=True, vmem_limit_bytes=48 * 2**20
        ),
        name="influence",
    )(train, query)


def solution(mesh):
    return jax.shard_map(
        body,
        mesh=mesh,
        in_specs=(P(("train", "query"), None, None), P(("query", "train"), None, None)),
        out_specs=P("train", "query"),
        check_vma=False,
    )
```
